128 devices in a mesh: band: 16 (over z, y_hi, core), ga: 8 (over y_lo, x).
Axes of the slice: x: 4, y: 4 (y_hi: 2, y_lo: 2; y = y_hi * 2 + y_lo), z: 4, core: 2. Of those that a mesh axis runs over, the one named last changes fastest.
Arguments:
- trial_bands: float32 [16, 2, 160, 5120], P('band', None, None, 'ga'), may hold values from -6 to 6
- basis_bands: float32 [16, 2, 160, 5120], P('band', None, None, 'ga'), may hold values from -6 to 6
- column_sites: int32 [5120], replicated, may hold values from 0 to 25599, as said below
- potential: float32 [160, 160, 160], P('ga'), may hold values from -1.5 to 0.5
- box_cells: int32 [1536, 128], P('ga'), may hold values from 0 to 511999, as said below
- box_atom: int32 [1536], P('ga'), may hold values from 0 to 1023, as said below
- box_beta: float32 [1536, 128], P('ga'), may hold values from -0.5 to 0.5
- strength: float32 [1024], replicated, may hold values from 2 to 8
Outputs:
- applied_bands: float32 [16, 2, 160, 5120], P('band', None, None, 'ga')
- gram_block: float32 [2, 16, 16], P(None, None, 'band')
The draws below stay inside these ranges and needn't reach their ends.
Inputs may be any that keep to these rules, and one draw needn't show every extreme that they name: `column_sites`: distinct positions; the first and the last position of a plane are among them. `box_cells`: each row is a box of 2 planes by 8 by 8 cells inside its device's own 20 planes, the in-plane indices wrapping around the grid; a cell is plane * 160 * 160 + x * 160 + y within that block of planes; entry j of a row is the cell at planes, x and y offsets (j // 64, (j // 8) % 8, j % 8) from the row's entry 0, x and y taken modulo 160. `box_atom`: an atom may own blocks on several devices or on none.
All inputs are finite; a program needn't handle non-finite values.
Results may differ from the reference program's by a relative error of at most 0.00011.
Values sent between devices are 32-bit elements; how exact they have to be, the bound alone decides.
No kernel may reach another device: no remote copies, remote signals or barrier semaphores. Data moves between devices by JAX's collectives and lax.ppermute only.
A program may use at most 192 MiB of HBM per device.

```python
import math
import jax
import jax.numpy as jnp
from jax import lax

GRID = 160
ZP = 20
NCOL = 5120
BANDS = 16
ATOMS = 1024
SLOTS = 192
BOXC = 128
N_GA = 8


def draw_column_sites(key, part):
    key = jax.random.fold_in(key, 11)
    key_perm, key_order = jax.random.split(key)
    plane_size = GRID * GRID
    middle = 1 + jax.random.permutation(key_perm, plane_size - 2)[:NCOL - 2]
    chosen = jnp.concatenate([jnp.array([0, plane_size - 1], dtype=jnp.int32), middle.astype(jnp.int32)])
    shuffle = jax.random.permutation(key_order, NCOL)
    return chosen[shuffle]


def draw_box_cells(key, part):
    key = jax.random.fold_in(key, 23)
    key_plane, key_row, key_col = jax.random.split(key, 3)
    total_rows = N_GA * SLOTS
    planes = GRID // N_GA
    zstart = jax.random.randint(key_plane, (total_rows,), 0, planes - 1)
    xstart = jax.random.randint(key_row, (total_rows,), 0, GRID)
    ystart = jax.random.randint(key_col, (total_rows,), 0, GRID)
    zstart = zstart.at[0].set(planes - 2).at[1].set(0)
    xstart = xstart.at[0].set(GRID - 8).at[1].set(0)
    ystart = ystart.at[0].set(GRID - 8).at[1].set(0)
    offset = jnp.arange(128, dtype=jnp.int32)
    step_z = offset // 64
    step_x = offset // 8 % 8
    step_y = offset % 8
    cell_index = (zstart[:, None] + step_z[None, :]) * (GRID * GRID) + (xstart[:, None] + step_x[None, :]) % GRID * GRID + (ystart[:, None] + step_y[None, :]) % GRID
    return cell_index.astype(jnp.int32)


def draw_box_atom(key, part):
    key = jax.random.fold_in(key, 37)
    atom_ids = jax.random.randint(key, (N_GA * SLOTS,), 0, ATOMS)
    return atom_ids.at[0].set(0).at[1].set(ATOMS - 1).astype(jnp.int32)


def levels(stream_key, extent, shards, low, largest):
    level = 1.0
    for position, parts in shards:
        steps = jax.random.uniform(jax.random.fold_in(jax.random.fold_in(stream_key, 6), position), (parts,), jnp.float32, low / len(shards), largest / len(shards))
        level = level * jnp.repeat(jnp.exp(steps), extent[position] // parts).reshape((-1,) + (1,) * (len(extent) - 1 - position))
    return level


def noise(stream_key, extent, width, reach, cuts=(), kind=jnp.bfloat16):
    values = jax.random.normal(stream_key, extent, jnp.float32) * width
    if len(cuts) > 0:
        values = levels(stream_key, extent, cuts, -0.22, 0.18) * values
    return jnp.clip(values, min=-reach, max=reach).astype(kind)


def setup_inputs(seed: int = 0) -> dict:
    key_of = jax.random.split(jax.random.key(seed), 9)
    return {
        "trial_bands": noise(key_of[0], (BANDS, 2, GRID, NCOL), 1.0, 6.0, ((0, 16), (3, 8)), jnp.float32),
        "basis_bands": noise(key_of[1], (BANDS, 2, GRID, NCOL), 1.0, 6.0, ((0, 16), (3, 8)), jnp.float32),
        "column_sites": draw_column_sites(jax.random.fold_in(key_of[8], 71), 0),
        "potential": jnp.clip(-1.5 + 2.0 * jax.random.uniform(key_of[3], (GRID, GRID, GRID), jnp.float32) ** levels(key_of[3], (GRID, GRID, GRID), ((0, 8),), -0.2, 0.2), -1.5, 0.5),
        "box_cells": draw_box_cells(jax.random.fold_in(key_of[8], 71), 0),
        "box_atom": draw_box_atom(jax.random.fold_in(key_of[8], 71), 0),
        "box_beta": noise(key_of[6], (SLOTS * N_GA, BOXC), BOXC ** -0.5, 0.5, ((0, 8),), jnp.float32),
        "strength": jnp.clip(jnp.exp(jax.random.uniform(key_of[7], (ATOMS,), jnp.float32, math.log(2.0), math.log(8.0))), 2.0, 8.0),
    }


highest = lax.Precision.HIGHEST

def frequency(index, length):
    return jnp.where(index < length // 2, index, index - length).astype(jnp.float32)

def reference(trial_bands, basis_bands, column_sites, potential, box_cells, box_atom, box_beta, strength):
    grid_total = float(GRID ** 3)
    axis_freq = frequency(jnp.arange(GRID, dtype=jnp.int32), GRID)
    freq_x = frequency(column_sites // GRID, GRID)
    freq_y = frequency(column_sites % GRID, GRID)
    kinetic = 2.0 * (axis_freq[:, None] ** 2 + freq_x[None, :] ** 2 + freq_y[None, :] ** 2) / float(GRID * GRID)
    owners = jnp.arange(SLOTS * N_GA, dtype=jnp.int32) // SLOTS
    global_cells = owners[:, None] * (ZP * GRID * GRID) + box_cells

    def apply_one(coeffs):
        spectral = lax.complex(coeffs[0], coeffs[1])
        grid_array = jnp.zeros((GRID, GRID * GRID), spectral.dtype).at[:, column_sites].set(spectral)
        real_field = jnp.fft.ifftn(grid_array.reshape(GRID, GRID, GRID)) * grid_total
        flat_field = real_field.reshape(-1)
        partial_value = lax.optimization_barrier(jnp.sum(flat_field[global_cells] * box_beta, axis=1))
        projected = jax.ops.segment_sum(partial_value, box_atom, num_segments=ATOMS)
        weights = (strength * projected)[box_atom]
        applied_field = (potential * real_field).reshape(-1).at[global_cells].add(weights[:, None] * box_beta)
        spectrum = jnp.fft.fftn(applied_field.reshape(GRID, GRID, GRID)) / grid_total
        picked = spectrum.reshape(GRID, GRID * GRID)[:, column_sites]
        result = picked + kinetic * spectral
        return jnp.stack([jnp.real(result), jnp.imag(result)])
    applied = lax.map(apply_one, trial_bands)
    real_sum = jnp.einsum('izc,jzc->ij', basis_bands[:, 0], applied[:, 0], precision=highest) + jnp.einsum('izc,jzc->ij', basis_bands[:, 1], applied[:, 1], precision=highest)
    imag_sum = jnp.einsum('izc,jzc->ij', basis_bands[:, 0], applied[:, 1], precision=highest) - jnp.einsum('izc,jzc->ij', basis_bands[:, 1], applied[:, 0], precision=highest)
    norm = 1.0 / math.sqrt(GRID * NCOL)
    gram_block = jnp.stack([real_sum, imag_sum]) * norm
    return (applied, gram_block)
```

```python
import math

import jax
import jax.numpy as jnp
import numpy as np
from jax import lax
from jax.experimental import pallas as pl
from jax.experimental.pallas import tpu as pltpu
from jax.sharding import PartitionSpec as P

N = 160
HALF = N // 2
N_GA = 8
PLANES = N // N_GA
NCOL = 5120
COLS = NCOL // N_GA
SLOTS = 192
ROWS_X = N + 8
LIMIT = 60 * 1024 * 1024
bf16 = jnp.bfloat16
f32 = jnp.float32


def split_np(matrix):
    high = np.asarray(matrix, np.float32).astype(jnp.bfloat16)
    low = (np.asarray(matrix, np.float64) - high.astype(np.float64)).astype(np.float32).astype(jnp.bfloat16)
    return high, low


def fourier(orient):
    index = np.arange(N)
    angle = (np.outer(index, index) % N) * (2.0 * np.pi / N)
    return np.cos(angle), orient * np.sin(angle)


def stage_matrix(orient, paired):
    cosine, sine = fourier(orient)
    if paired:
        order = np.concatenate([np.arange(0, N, 2), np.arange(1, N, 2)])
        cosine, sine = cosine[:, order], sine[:, order]
    ch, cl = split_np(cosine)
    sh, sl = split_np(sine)
    return np.concatenate([ch, sh, ch, sh, cl, sl], axis=1)


def sent_order():
    rows = []
    for d in range(N_GA):
        for part, span in ((0, range(16)), (1, range(16)), (0, range(16, 20)), (1, range(16, 20))):
            rows += [(part, d * PLANES + p) for p in span]
    return rows


def depth_matrices():
    cosine, sine = fourier(1.0)
    full = np.block([[cosine, -sine], [sine, cosine]])
    back = np.block([[cosine, sine], [-sine, cosine]]) / float(N**3)
    order = np.array([part * N + z for part, z in sent_order()])
    return full[order].astype(np.float32), back[:, order].astype(np.float32)


def lanes():
    return lax.broadcasted_iota(jnp.int32, (1, 128), 1)


def fourier_rows(matrix, blocks):
    lane = lanes()
    sign = jnp.where(lane < 64, -1.0, 1.0).astype(f32)
    pieces = []
    for block in blocks:
        turned = pltpu.roll(block, 64, 1) * sign
        high = block.astype(bf16)
        low = (block - high.astype(f32)).astype(bf16)
        turned_high = turned.astype(bf16)
        turned_low = (turned - turned_high.astype(f32)).astype(bf16)
        pieces.append(jnp.concatenate([high, turned_high, low, turned_low, high, turned_high], axis=0))
    right = pieces[0] if len(pieces) == 1 else jnp.concatenate(pieces, axis=1)
    return jnp.dot(matrix, right, preferred_element_type=f32)


def exchange_pairs(first, second):
    odd = (lanes() // 32) % 2 == 1
    even_rows = jnp.where(odd, pltpu.roll(second, 32, 1), first)
    odd_rows = jnp.where(odd, second, pltpu.roll(first, 96, 1))
    return jnp.concatenate([even_rows, odd_rows], axis=0)


def forward_kernel(
    site_row, box_row, recv, first_matrix, second_matrix, potential, beta, applied, partial, grid, mixed, stage, sums
):
    def transpose(t, carry):
        d = t // 5
        start = pl.multiple_of((t % 5) * 128, 128)
        block = recv[d, :, pl.ds(start, 128)]
        real, imag, rest = block[0:16], block[16:32], block[32:40]
        swapped = pltpu.roll(rest, 4, 0)
        zero = jnp.zeros((8, 128), f32)
        stacked = jnp.concatenate(
            [real, rest, zero, real, rest, zero, imag, swapped, zero, imag, swapped, zero], axis=0
        )
        stage[pl.ds(pl.multiple_of(t * 128, 128), 128), :] = stacked.T
        return carry

    lax.fori_loop(0, NCOL // 128, transpose, 0)

    def clear(t, carry):
        grid[pl.ds(pl.multiple_of(t * 256, 256), 256), :] = jnp.zeros((256, 128), f32)
        return carry

    lax.fori_loop(0, N * N // 256, clear, 0)

    def place(t, carry):
        base = t * 16
        for k in range(16):
            grid[pl.ds(site_row[base + k], 1), :] = stage[pl.ds(base + k, 1), :]
        return carry

    lax.fori_loop(0, NCOL // 16, place, 0)

    odd = (lanes() // 32) % 2 == 1

    def along_x(t, carry):
        blocks = []
        for k in range(2):
            start = pl.multiple_of((t * 2 + k) * 2 * N, 16)
            even_y = grid[pl.ds(start, N), :]
            odd_y = grid[pl.ds(start + N, N), :]
            blocks.append(jnp.where(odd, odd_y, even_y))
        result = fourier_rows(first_matrix[...], blocks)
        for k in range(2):
            mixed[t * 2 + k] = result[:, k * 128 : (k + 1) * 128]
        return carry

    lax.fori_loop(0, HALF // 2, along_x, 0)

    def along_y(t, carry):
        blocks = []
        for k in range(2):
            pair = t * 2 + k
            blocks.append(exchange_pairs(mixed[:, 2 * pair, :], mixed[:, 2 * pair + 1, :]))
        result = fourier_rows(second_matrix[...], blocks)
        for k in range(2):
            pair = t * 2 + k
            values = result[:, k * 128 : (k + 1) * 128]
            start = pl.multiple_of(pair * ROWS_X, 8)
            grid[pl.ds(start, N), :] = values
            grid[pl.ds(start + N, 8), :] = values[0:8]
            applied[pl.ds(start, N), :] = values * potential[pl.ds(pl.multiple_of(pair * N, 16), N), :]
            applied[pl.ds(start + N, 8), :] = jnp.zeros((8, 128), f32)
        return carry

    lax.fori_loop(0, HALF // 2, along_y, 0)

    def project(t, carry):
        for k in range(4):
            s = t * 4 + k
            total = jnp.zeros((8, 128), f32)
            for i in range(5):
                weight = beta[pl.ds(pl.multiple_of(s * 40 + i * 8, 8), 8), :]
                total = total + weight * grid[pl.ds(box_row[s * 5 + i], 8), :]
            sums[pl.ds(pl.multiple_of(s * 8, 8), 8), :] = total
        return carry

    lax.fori_loop(0, SLOTS // 4, project, 0)
    totals = jnp.sum(sums[...].reshape(SLOTS, 8, 128), axis=1)
    row = lax.broadcasted_iota(jnp.int32, (8, 128), 0)
    column = lax.broadcasted_iota(jnp.int32, (8, 128), 1)
    chooser = jnp.where(row == column // 64, 1.0, 0.0).astype(f32)
    partial[...] = lax.dot_general(
        chooser, totals, (((1,), (1,)), ((), ())), precision=lax.Precision.HIGHEST, preferred_element_type=f32
    )


def backward_kernel(
    site_row, box_row, weights, applied_in, beta, first_matrix, second_matrix, parity, sent, applied, mixed, grid, stage
):
    lane = lanes()

    def add_boxes(s, carry):
        weight = jnp.where(lane < 64, weights[0, s], weights[1, s])
        for i in range(5):
            start = box_row[s * 5 + i]
            extra = beta[pl.ds(pl.multiple_of(s * 40 + i * 8, 8), 8), :] * weight
            applied[pl.ds(start, 8), :] = applied[pl.ds(start, 8), :] + extra
        return carry

    applied[...] = applied_in[...]
    lax.fori_loop(0, SLOTS, add_boxes, 0)

    def along_y(t, carry):
        blocks = []
        for k in range(2):
            start = pl.multiple_of((t * 2 + k) * ROWS_X, 8)
            top = applied[pl.ds(start, 8), :] + applied[pl.ds(start + N, 8), :]
            blocks.append(jnp.concatenate([top, applied[pl.ds(start + 8, N - 8), :]], axis=0))
        result = fourier_rows(first_matrix[...], blocks)
        for k in range(2):
            mixed[t * 2 + k] = result[:, k * 128 : (k + 1) * 128]
        return carry

    lax.fori_loop(0, HALF // 2, along_y, 0)

    def along_x(t, carry):
        blocks = []
        for k in range(2):
            pair = t * 2 + k
            blocks.append(exchange_pairs(mixed[:, 2 * pair, :], mixed[:, 2 * pair + 1, :]))
        result = fourier_rows(second_matrix[...], blocks)
        for k in range(2):
            grid[pl.ds(pl.multiple_of((t * 2 + k) * N, 16), N), :] = result[:, k * 128 : (k + 1) * 128]
        return carry

    lax.fori_loop(0, HALF // 2, along_x, 0)

    def pick(t, carry):
        base = t * 16
        for k in range(16):
            stage[pl.ds(base + k, 1), :] = grid[pl.ds(site_row[base + k], 1), :]
        return carry

    lax.fori_loop(0, NCOL // 16, pick, 0)

    def transpose(t, carry):
        d = t // 5
        start = pl.multiple_of((t % 5) * 128, 128)
        turned = stage[pl.ds(pl.multiple_of(t * 128, 128), 128), :].T
        is_odd = parity[pl.ds(t, 1), :] > 0
        real = jnp.where(is_odd, turned[32:56], turned[0:24])
        imag = jnp.where(is_odd, turned[96:120], turned[64:88])
        upper = lax.broadcasted_iota(jnp.int32, (8, 128), 0) < 4
        rest = jnp.where(upper, real[16:24], pltpu.roll(imag[16:24], 4, 0))
        sent[d, :, pl.ds(start, 128)] = jnp.concatenate([real[0:16], imag[0:16], rest], axis=0)
        return carry

    lax.fori_loop(0, NCOL // 128, transpose, 0)


def whole(space=pltpu.VMEM):
    return pl.BlockSpec(memory_space=space)


def frequency(index):
    return jnp.where(index < HALF, index, index - N).astype(f32)


def box_tables(box_cells, box_atom, box_beta):
    corner = box_cells[:, 0]
    plane = corner // (N * N)
    row = corner // N % N
    col = corner % N
    pair = (row[:, None] // 2 + jnp.arange(5, dtype=jnp.int32)[None, :]) % HALF
    box_row = (pair * ROWS_X + col[:, None]).reshape(-1)
    values = box_beta.reshape(SLOTS, 2, 8, 8)
    even = jnp.pad(values, ((0, 0), (0, 0), (0, 2), (0, 0)))
    shifted = jnp.pad(values, ((0, 0), (0, 0), (1, 1), (0, 0)))
    chosen = jnp.where((row % 2 == 0)[:, None, None, None], even, shifted)
    chosen = chosen.reshape(SLOTS, 2, 5, 2, 8)
    lane = jnp.arange(128, dtype=jnp.int32)
    lane_half = lane // 32 % 2
    lane_plane = lane % 32
    low = jnp.where(lane_half == 0, chosen[:, 0, :, 0, :, None], chosen[:, 0, :, 1, :, None])
    high = jnp.where(lane_half == 0, chosen[:, 1, :, 0, :, None], chosen[:, 1, :, 1, :, None])
    at = plane[:, None, None, None]
    table = jnp.where(lane_plane == at, low, 0.0) + jnp.where(lane_plane == at + 1, high, 0.0)
    return box_row, table.reshape(SLOTS * 40, 128)


def potential_rows(potential):
    turned = potential.reshape(PLANES, HALF, 2, N).transpose(1, 3, 2, 0)
    padded = jnp.pad(turned, ((0, 0), (0, 0), (0, 0), (0, 12))).reshape(HALF * N, 64)
    return jnp.concatenate([padded, padded], axis=1)


def on_device(trial_bands, basis_bands, column_sites, potential, box_cells, box_atom, box_beta, strength):
    forward_depth, backward_depth = depth_matrices()
    trial = trial_bands.reshape(2 * N, COLS)
    high3 = lax.Precision.HIGH
    basis_all = lax.all_gather(basis_bands, "band", axis=0, tiled=True)
    depth = jnp.dot(jnp.asarray(forward_depth), trial, precision=high3).reshape(N_GA, 40, COLS)
    atoms_all = lax.all_gather(box_atom, "ga", axis=0, tiled=True)
    recv = lax.all_to_all(depth, "ga", split_axis=0, concat_axis=0, tiled=True)

    site_x = column_sites // N
    site_y = column_sites % N
    box_row, beta = box_tables(box_cells, box_atom, box_beta)
    pot = potential_rows(potential)
    row_count = HALF * ROWS_X
    applied, partial = pl.pallas_call(
        forward_kernel,
        out_shape=(
            jax.ShapeDtypeStruct((row_count, 128), f32),
            jax.ShapeDtypeStruct((8, SLOTS), f32),
        ),
        in_specs=[whole(pltpu.SMEM), whole(pltpu.SMEM)] + [whole()] * 5,
        out_specs=(whole(), whole()),
        scratch_shapes=[
            pltpu.VMEM((N * N, 128), f32),
            pltpu.VMEM((HALF, N, 128), f32),
            pltpu.VMEM((NCOL, 128), f32),
            pltpu.VMEM((SLOTS * 8, 128), f32),
        ],
        compiler_params=pltpu.CompilerParams(vmem_limit_bytes=LIMIT),
        name="planes_forward",
    )(
        site_y * N + site_x,
        box_row,
        recv,
        jnp.asarray(stage_matrix(1.0, False)),
        jnp.asarray(stage_matrix(1.0, True)),
        pot,
        beta,
    )
    same = (atoms_all[:, None] == box_atom[None, :]).astype(f32) * strength[box_atom][None, :]
    copies = jnp.broadcast_to(partial[None, :2], (N_GA, 2, SLOTS))
    shared = lax.all_to_all(copies, "ga", split_axis=0, concat_axis=0, tiled=True)
    shared = shared.transpose(1, 0, 2).reshape(2, N_GA * SLOTS)
    weights = jnp.dot(shared, same, precision=lax.Precision.HIGHEST)
    sent = pl.pallas_call(
        backward_kernel,
        out_shape=jax.ShapeDtypeStruct((N_GA, 40, COLS), f32),
        in_specs=[whole(pltpu.SMEM)] * 3 + [whole()] * 5,
        out_specs=whole(),
        scratch_shapes=[
            pltpu.VMEM((row_count, 128), f32),
            pltpu.VMEM((HALF, N, 128), f32),
            pltpu.VMEM((HALF * N, 128), f32),
            pltpu.VMEM((NCOL, 128), f32),
        ],
        compiler_params=pltpu.CompilerParams(vmem_limit_bytes=LIMIT),
        name="planes_backward",
    )(
        (site_y // 2) * N + site_x,
        box_row,
        weights,
        applied,
        beta,
        jnp.asarray(stage_matrix(-1.0, False)),
        jnp.asarray(stage_matrix(-1.0, True)),
        (site_y % 2).reshape(NCOL // 128, 128),
    )
    returned = lax.all_to_all(sent, "ga", split_axis=0, concat_axis=0, tiled=True)
    spectrum = jnp.dot(jnp.asarray(backward_depth), returned.reshape(2 * N, COLS), precision=high3)
    own = lax.dynamic_slice_in_dim(column_sites, lax.axis_index("ga") * COLS, COLS)
    fz = frequency(jnp.arange(N, dtype=jnp.int32))
    kinetic = (2.0 / float(N * N)) * (
        fz[:, None] ** 2 + frequency(own // N)[None, :] ** 2 + frequency(own % N)[None, :] ** 2
    )
    result = spectrum.reshape(2, N, COLS) + kinetic * trial.reshape(2, N, COLS)
    real_sum = jnp.sum(basis_all * result[None], axis=(1, 2, 3))
    imag_sum = jnp.sum(basis_all[:, 0] * result[None, 1] - basis_all[:, 1] * result[None, 0], axis=(1, 2))
    partial_gram = jnp.stack([real_sum, imag_sum]) * (1.0 / math.sqrt(N * NCOL))
    copies = jnp.broadcast_to(partial_gram[None], (N_GA, 2, 16))
    gram = jnp.sum(lax.all_to_all(copies, "ga", split_axis=0, concat_axis=0, tiled=True), axis=0)
    return (result[None], gram[:, :, None])


def solution(mesh):
    placed = (
        P("band", None, None, "ga"),
        P("band", None, None, "ga"),
        P(),
        P("ga", None, None),
        P("ga", None),
        P("ga"),
        P("ga", None),
        P(),
    )
    return jax.shard_map(
        on_device,
        mesh=mesh,
        in_specs=placed,
        out_specs=(P("band", None, None, "ga"), P(None, None, "band")),
        check_vma=False,
    )
```

```python
import math

import jax
import jax.numpy as jnp
import numpy as np
from jax import lax
from jax.experimental import pallas as pl
from jax.experimental.pallas import tpu as pltpu
from jax.sharding import PartitionSpec as P

N = 160
HALF = N // 2
N_GA = 8
PLANES = N // N_GA
NCOL = 5120
COLS = NCOL // N_GA
SLOTS = 192
ROWS_X = N + 8
ATOMS = 1024
GROUP = 40
PITCH = 164
LIMIT = 60 * 1024 * 1024
bf16 = jnp.bfloat16
f32 = jnp.float32


def split_np(matrix):
    high = np.asarray(matrix, np.float32).astype(jnp.bfloat16)
    low = (np.asarray(matrix, np.float64) - high.astype(np.float64)).astype(np.float32).astype(jnp.bfloat16)
    return high, low


def fourier(orient):
    index = np.arange(N)
    angle = (np.outer(index, index) % N) * (2.0 * np.pi / N)
    return np.cos(angle), orient * np.sin(angle)


def stage_matrix(orient, paired):
    cosine, sine = fourier(orient)
    if paired:
        order = np.concatenate([np.arange(0, N, 2), np.arange(1, N, 2)])
        cosine, sine = cosine[:, order], sine[:, order]
    ch, cl = split_np(cosine)
    sh, sl = split_np(sine)
    return np.concatenate([ch, sh, ch, sh, cl, sl], axis=1)


def sent_order():
    rows = []
    for d in range(N_GA):
        for part, span in ((0, range(16)), (1, range(16)), (0, range(16, 20)), (1, range(16, 20))):
            rows += [(part, d * PLANES + p) for p in span]
    return rows


def depth_matrices():
    cosine, sine = fourier(1.0)
    full = np.block([[cosine, -sine], [sine, cosine]])
    back = np.block([[cosine, sine], [-sine, cosine]]) / float(N**3)
    order = np.array([part * N + z for part, z in sent_order()])
    tables = []
    for matrix in (full[order], back[:, order]):
        high, low = split_np(matrix)
        tables.append(np.concatenate([high, high, low], axis=1))
    return tables


def lanes():
    return lax.broadcasted_iota(jnp.int32, (1, 128), 1)


def fourier_rows(matrix, blocks):
    lane = lanes()
    sign = jnp.where(lane < 64, -1.0, 1.0).astype(f32)
    pieces = []
    for block in blocks:
        turned = pltpu.roll(block, 64, 1) * sign
        high = block.astype(bf16)
        low = (block - high.astype(f32)).astype(bf16)
        turned_high = turned.astype(bf16)
        turned_low = (turned - turned_high.astype(f32)).astype(bf16)
        pieces.append(jnp.concatenate([high, turned_high, low, turned_low, high, turned_high], axis=0))
    right = pieces[0] if len(pieces) == 1 else jnp.concatenate(pieces, axis=1)
    return jnp.dot(matrix, right, preferred_element_type=f32)


def exchange_pairs(first, second):
    odd = (lanes() // 32) % 2 == 1
    even_rows = jnp.where(odd, pltpu.roll(second, 32, 1), first)
    odd_rows = jnp.where(odd, second, pltpu.roll(first, 96, 1))
    return jnp.concatenate([even_rows, odd_rows], axis=0)


def split3(values):
    high = values.astype(bf16)
    rest = values - high.astype(f32)
    middle = rest.astype(bf16)
    return high, middle, (rest - middle.astype(f32)).astype(bf16)


def exact_dot(first, second, contract):
    total = None
    if isinstance(first, tuple):
        terms = [(piece, second) for piece in first]
    else:
        terms = [(first, piece) for piece in second]
    for left, right in terms:
        product = lax.dot_general(left, right, (contract, ((), ())), preferred_element_type=f32)
        total = product if total is None else total + product
    return total


def atom_table(atoms):
    row = lax.broadcasted_iota(jnp.int32, (ATOMS, SLOTS), 0)
    return jnp.where(atoms[...] == row, 1.0, 0.0).astype(bf16)


def box_places(box_base, s):
    places = []
    for i in range(5):
        start = box_base[s] + i * ROWS_X
        places.append(pl.ds(jnp.where(start >= HALF * ROWS_X, start - HALF * ROWS_X, start), 8))
    return places


def depth_product(matrix, values):
    high = values.astype(bf16)
    low = (values - high.astype(f32)).astype(bf16)
    return jnp.dot(matrix, jnp.concatenate([high, low, high], axis=0), preferred_element_type=f32)


def depth_kernel(matrix, values, out):
    out[...] = depth_product(matrix[...], values[...])


def prepare_kernel(
    box_plane, box_odd, potential, box_beta, potential_out, beta_out, rows, table, sems
):
    copies = []

    def send(source, target, start, size):
        span = pl.ds(start, size)
        copies.append(pltpu.make_async_copy(source.at[span], target.at[span], sems.at[len(copies)]))
        copies[-1].start()

    lane = lanes()
    lane_odd = (lane // 32) % 2 == 1
    lane_plane = lane % 32
    local_box = lax.broadcasted_iota(jnp.int32, (16, 128), 0) % 8
    local_plane = lane_plane - lax.broadcasted_iota(jnp.int32, (16, 128), 0) // 8
    nothing = jnp.zeros((8, 128), f32)

    def spread(t, carry):
        values = box_beta[pl.ds(pl.multiple_of(t * 8, 8), 8), :]
        both = jnp.concatenate([values, pltpu.roll(values, 64, 1)], axis=0)
        high = both.astype(bf16).astype(f32)
        left = jnp.concatenate([high, both - high], axis=0).T[0:64].astype(bf16)
        masks = []
        for k in range(8):
            hit = (local_box == k) & (local_plane == box_plane[t * 8 + k])
            masks.append(jnp.where(hit, 1.0, 0.0))
        mask = jnp.concatenate(masks, axis=1)
        right = jnp.concatenate([mask, mask], axis=0).astype(bf16)
        lines = jnp.dot(left, right, preferred_element_type=f32)
        for k in range(8):
            s = t * 8 + k
            shifted = box_odd[s] > 0
            line = [lines[x * 8 : x * 8 + 8, k * 128 : (k + 1) * 128] for x in range(8)]
            for i in range(5):
                even = line[2 * i] if i < 4 else nothing
                straight = jnp.where(lane_odd, line[2 * i + 1], even) if i < 4 else nothing
                moved = jnp.where(lane_odd, even, line[2 * i - 1] if i > 0 else nothing)
                table[pl.ds(pl.multiple_of(s * 40 + i * 8, 8), 8), :] = jnp.where(shifted, moved, straight)
        return carry

    def spread_two(t, carry):
        spread(2 * t, 0)
        spread(2 * t + 1, 0)
        return carry

    for piece in range(2):
        lax.fori_loop(piece * 6, piece * 6 + 6, spread_two, 0)
        send(table, beta_out, piece * SLOTS * 20, SLOTS * 20)
    zero = jnp.zeros((8, N), f32)
    for piece in range(4):
        for k in range(HALF // 4):
            pair = piece * (HALF // 4) + k
            pieces = []
            for half in range(2):
                plane = potential[:, 2 * pair + half, :]
                pieces += [plane[0:8], plane[8:16], jnp.concatenate([plane[16:20], zero[0:4]], axis=0), zero]
            stacked = jnp.concatenate(pieces + pieces, axis=0)
            rows[pair * N : pair * N + 128, :] = stacked[:, 0:128].T
            rows[pair * N + 128 : pair * N + N, :] = stacked[:, 128:N].T
        send(rows, potential_out, piece * (HALF // 4) * N, (HALF // 4) * N)
    for copy in copies:
        copy.wait()


def finish_kernel(
    matrix, returned, trial, plane_kinetic, basis_all, result, gram, basis, sums, sems
):
    pairs = basis_all.shape[0] // 2

    def brought(m):
        span = pl.ds(2 * m, 2)
        return pltpu.make_async_copy(basis_all.at[span], basis.at[span], sems.at[m])

    for m in range(pairs):
        brought(m).start()
    depth = lax.broadcasted_iota(jnp.int32, (N, 1), 0)
    depth = jnp.where(depth < HALF, depth, depth - N).astype(f32)
    kinetic = (2.0 / float(N * N)) * (depth * depth) + plane_kinetic[...]
    spectrum = depth_product(matrix[...], returned[...])
    result[0:N, :] = spectrum[0:N] + kinetic * trial[0:N, :]
    result[N : 2 * N, :] = spectrum[N : 2 * N] + kinetic * trial[N : 2 * N, :]

    def one_pair(m, carry):
        brought(m).wait()

        def rows(t, totals):
            totals = list(totals)
            for k in range(4):
                real_at = pl.ds(pl.multiple_of(t * 32 + k * 8, 8), 8)
                imag_at = pl.ds(pl.multiple_of(N + t * 32 + k * 8, 8), 8)
                real, imag = result[real_at, :], result[imag_at, :]
                for n in range(2):
                    left_real, left_imag = basis[2 * m + n, real_at, :], basis[2 * m + n, imag_at, :]
                    totals[2 * n] = totals[2 * n] + (left_real * real + left_imag * imag)
                    totals[2 * n + 1] = totals[2 * n + 1] + (left_real * imag - left_imag * real)
            return tuple(totals)

        totals = lax.fori_loop(0, N // 32, rows, (jnp.zeros((8, COLS), f32),) * 4)
        for n, total in enumerate(totals):
            line = jnp.sum(total, axis=0, keepdims=True)
            short = line[:, 0:128]
            for j in range(1, COLS // 128):
                short = short + line[:, j * 128 : (j + 1) * 128]
            sums[pl.ds(m * 4 + n, 1), :] = short
        return carry

    lax.fori_loop(0, pairs, one_pair, 0)
    gram[...] = exact_dot(jnp.ones((8, 128), bf16), split3(sums[...]), ((1,), (1,)))


def forward_kernel(
    site_row, box_base, recv, first_matrix, second_matrix, atoms, potential_in, beta_in,
    applied_out, shared, grid, mixed, stage, sums, applied, potential, beta, sems,
):
    potential_copy = pltpu.make_async_copy(potential_in, potential, sems.at[0])
    beta_copy = pltpu.make_async_copy(beta_in, beta, sems.at[1])
    potential_copy.start()
    beta_copy.start()

    def transpose(d, carry):
        for j in range(COLS // 128):
            block = recv[d, :, j * 128 : (j + 1) * 128]
            real, imag, rest = block[0:16], block[16:32], block[32:40]
            swapped = pltpu.roll(rest, 4, 0)
            zero = jnp.zeros((8, 128), f32)
            stacked = jnp.concatenate(
                [real, rest, zero, real, rest, zero, imag, swapped, zero, imag, swapped, zero], axis=0
            )
            stage[pl.ds(pl.multiple_of(d * COLS + j * 128, 128), 128), :] = stacked.T
        return carry

    lax.fori_loop(0, N_GA, transpose, 0)

    def clear(t, carry):
        grid[pl.ds(pl.multiple_of(t * 256, 256), 256), :] = jnp.zeros((256, 128), f32)
        return carry

    lax.fori_loop(0, N * N // 256, clear, 0)

    def place(t, carry):
        base = t * 64
        for k in range(64):
            grid[pl.ds(site_row[base + k], 1), :] = stage[pl.ds(base + k, 1), :]
        return carry

    lax.fori_loop(0, NCOL // 64, place, 0)

    odd = (lanes() // 32) % 2 == 1

    def along_x(t, carry):
        blocks = []
        for k in range(GROUP):
            start = pl.multiple_of((t * GROUP + k) * 2 * N, 16)
            even_y = grid[pl.ds(start, N), :]
            odd_y = grid[pl.ds(start + N, N), :]
            blocks.append(jnp.where(odd, odd_y, even_y))
        result = fourier_rows(first_matrix[...], blocks)
        for k in range(GROUP):
            mixed[pl.ds((t * GROUP + k) * PITCH, N), :] = result[:, k * 128 : (k + 1) * 128]
        return carry

    lax.fori_loop(0, HALF // GROUP, along_x, 0)
    potential_copy.wait()

    def along_y(t, carry):
        blocks = []
        for k in range(GROUP):
            pair = t * GROUP + k
            blocks.append(
                exchange_pairs(
                    mixed[pl.ds(2 * pair, HALF, stride=PITCH), :], mixed[pl.ds(2 * pair + 1, HALF, stride=PITCH), :]
                )
            )
        result = fourier_rows(second_matrix[...], blocks)
        for k in range(GROUP):
            pair = t * GROUP + k
            values = result[:, k * 128 : (k + 1) * 128]
            start = pl.multiple_of(pair * ROWS_X, 8)
            grid[pl.ds(start, N), :] = values
            grid[pl.ds(start + N, 8), :] = values[0:8]
            applied[pl.ds(start, N), :] = values * potential[pl.ds(pl.multiple_of(pair * N, 16), N), :]
            applied[pl.ds(start + N, 8), :] = jnp.zeros((8, 128), f32)
        return carry

    copies = []
    for t in range(HALF // GROUP):
        along_y(t, 0)
        piece = pl.ds(t * GROUP * ROWS_X, GROUP * ROWS_X)
        copy = pltpu.make_async_copy(applied.at[piece], applied_out.at[piece], sems.at[2 + t])
        copy.start()
        copies.append(copy)
    beta_copy.wait()

    def project(t, carry):
        for k in range(4):
            s = t * 4 + k
            total = jnp.zeros((8, 128), f32)
            for i, place in enumerate(box_places(box_base, s)):
                weight = beta[pl.ds(pl.multiple_of(s * 40 + i * 8, 8), 8), :]
                total = total + weight * grid[place, :]
            sums[pl.ds(pl.multiple_of(s * 8, 8), 8), :] = total
        return carry

    lax.fori_loop(0, SLOTS // 4, project, 0)
    totals = jnp.sum(sums[...].reshape(SLOTS, 8, 128), axis=1)
    row = lax.broadcasted_iota(jnp.int32, (8, 128), 0)
    column = lax.broadcasted_iota(jnp.int32, (8, 128), 1)
    chooser = jnp.where(row == column // 64, 1.0, 0.0).astype(bf16)
    partial = exact_dot(chooser, split3(totals), ((1,), (1,)))
    by_atom = exact_dot(split3(partial), atom_table(atoms), ((1,), (1,)))
    for part in range(2):
        for r in range(4):
            values = by_atom[part : part + 1, r * 256 : (r + 1) * 256]
            for d in range(N_GA):
                shared[d, part * 4 + r : part * 4 + r + 1, :] = values
    for copy in copies:
        copy.wait()


def backward_kernel(
    site_row, box_base, shared, strength, atoms, first_matrix, second_matrix, parity, applied_in, beta_in,
    sent, applied, mixed, grid, stage, beta, weights, sems,
):
    applied_copy = pltpu.make_async_copy(applied_in, applied, sems.at[0])
    beta_copy = pltpu.make_async_copy(beta_in, beta, sems.at[1])
    applied_copy.start()
    beta_copy.start()
    total = jnp.sum(shared[...], axis=0)
    by_part = []
    for part in range(2):
        whole_row = jnp.concatenate([total[part * 4 + r : part * 4 + r + 1, :] for r in range(4)], axis=1)
        by_part.append(jnp.broadcast_to(whole_row * strength[...], (64, ATOMS)))
    spread = jnp.concatenate(by_part, axis=0)
    weights[...] = exact_dot(split3(spread), atom_table(atoms), ((1,), (0,))).T
    applied_copy.wait()
    beta_copy.wait()

    def add_boxes(t, carry):
        for k in range(2):
            s = t * 2 + k
            weight = weights[pl.ds(s, 1), :]
            places = box_places(box_base, s)
            olds = [applied[place, :] for place in places]
            for i in range(5):
                applied[places[i], :] = olds[i] + beta[pl.ds(pl.multiple_of(s * 40 + i * 8, 8), 8), :] * weight
        return carry

    lax.fori_loop(0, SLOTS // 2, add_boxes, 0)

    def along_y(t, carry):
        blocks = []
        for k in range(GROUP):
            start = pl.multiple_of((t * GROUP + k) * ROWS_X, 8)
            top = applied[pl.ds(start, 8), :] + applied[pl.ds(start + N, 8), :]
            blocks.append(jnp.concatenate([top, applied[pl.ds(start + 8, N - 8), :]], axis=0))
        result = fourier_rows(first_matrix[...], blocks)
        for k in range(GROUP):
            mixed[pl.ds((t * GROUP + k) * PITCH, N), :] = result[:, k * 128 : (k + 1) * 128]
        return carry

    lax.fori_loop(0, HALF // GROUP, along_y, 0)

    def along_x(t, carry):
        blocks = []
        for k in range(GROUP):
            pair = t * GROUP + k
            blocks.append(
                exchange_pairs(
                    mixed[pl.ds(2 * pair, HALF, stride=PITCH), :], mixed[pl.ds(2 * pair + 1, HALF, stride=PITCH), :]
                )
            )
        result = fourier_rows(second_matrix[...], blocks)
        for k in range(GROUP):
            grid[pl.ds(pl.multiple_of((t * GROUP + k) * N, 16), N), :] = result[:, k * 128 : (k + 1) * 128]
        return carry

    lax.fori_loop(0, HALF // GROUP, along_x, 0)

    def pick(t, carry):
        base = t * 64
        for k in range(64):
            stage[pl.ds(base + k, 1), :] = grid[pl.ds(site_row[base + k], 1), :]
        return carry

    lax.fori_loop(0, NCOL // 64, pick, 0)
    upper = lax.broadcasted_iota(jnp.int32, (8, 128), 0) < 4

    def transpose(d, carry):
        for j in range(COLS // 128):
            turned = stage[pl.ds(pl.multiple_of(d * COLS + j * 128, 128), 128), :].T
            is_odd = parity[pl.ds(d * (COLS // 128) + j, 1), :] > 0
            real = jnp.where(is_odd, turned[32:56], turned[0:24])
            imag = jnp.where(is_odd, turned[96:120], turned[64:88])
            rest = jnp.where(upper, real[16:24], pltpu.roll(imag[16:24], 4, 0))
            sent[d, :, j * 128 : (j + 1) * 128] = jnp.concatenate([real[0:16], imag[0:16], rest], axis=0)
        return carry

    lax.fori_loop(0, N_GA, transpose, 0)


def whole(space=pltpu.VMEM):
    return pl.BlockSpec(memory_space=space)


def frequency(index):
    return jnp.where(index < HALF, index, index - N).astype(f32)


def on_device(trial_bands, basis_bands, column_sites, potential, box_cells, box_atom, box_beta, strength):
    forward_depth, backward_depth = depth_matrices()
    bands = lax.axis_size("band")
    basis_all = lax.all_gather(basis_bands.reshape(2 * N, COLS), "band", axis=0)
    trial = trial_bands.reshape(2 * N, COLS)
    depth = pl.pallas_call(
        depth_kernel,
        out_shape=jax.ShapeDtypeStruct((2 * N, COLS), f32),
        in_specs=[whole()] * 2,
        out_specs=whole(),
        compiler_params=pltpu.CompilerParams(vmem_limit_bytes=LIMIT),
        name="depth",
    )(jnp.asarray(forward_depth), trial)
    recv = lax.all_to_all(depth.reshape(N_GA, 40, COLS), "ga", split_axis=0, concat_axis=0, tiled=True)

    site_x = column_sites // N
    site_y = column_sites - site_x * N
    corner = box_cells[:, 0]
    corner_plane = corner // (N * N)
    in_plane = corner - corner_plane * (N * N)
    corner_x = in_plane // N
    box_base = (corner_x // 2) * ROWS_X + (in_plane - corner_x * N)
    pot, beta = pl.pallas_call(
        prepare_kernel,
        out_shape=(
            jax.ShapeDtypeStruct((HALF * N, 128), f32),
            jax.ShapeDtypeStruct((SLOTS * 40, 128), f32),
        ),
        in_specs=[whole(pltpu.SMEM)] * 2 + [whole()] * 2,
        out_specs=(whole(pl.ANY), whole(pl.ANY)),
        scratch_shapes=[
            pltpu.VMEM((HALF * N, 128), f32),
            pltpu.VMEM((SLOTS * 40, 128), f32),
            pltpu.SemaphoreType.DMA((6,)),
        ],
        compiler_params=pltpu.CompilerParams(vmem_limit_bytes=LIMIT),
        cost_estimate=pl.CostEstimate(flops=0, bytes_accessed=14000000, transcendentals=0),
        name="prepare",
    )(corner_plane, corner_x % 2, potential, box_beta)
    row_count = HALF * ROWS_X
    applied, shared = pl.pallas_call(
        forward_kernel,
        out_shape=(
            jax.ShapeDtypeStruct((row_count, 128), f32),
            jax.ShapeDtypeStruct((N_GA, 8, ATOMS // 4), f32),
        ),
        in_specs=[whole(pltpu.SMEM)] * 2 + [whole()] * 4 + [whole(pl.ANY)] * 2,
        out_specs=(whole(pl.ANY), whole()),
        scratch_shapes=[
            pltpu.VMEM((N * N, 128), f32),
            pltpu.VMEM((HALF * PITCH, 128), f32),
            pltpu.VMEM((NCOL, 128), f32),
            pltpu.VMEM((SLOTS * 8, 128), f32),
            pltpu.VMEM((row_count, 128), f32),
            pltpu.VMEM((HALF * N, 128), f32),
            pltpu.VMEM((SLOTS * 40, 128), f32),
            pltpu.SemaphoreType.DMA((2 + HALF // GROUP,)),
        ],
        compiler_params=pltpu.CompilerParams(vmem_limit_bytes=LIMIT),
        name="planes_forward",
    )(
        site_y * N + site_x,
        box_base,
        recv,
        jnp.asarray(stage_matrix(1.0, False)),
        jnp.asarray(stage_matrix(1.0, True)),
        box_atom.reshape(1, SLOTS),
        pot,
        beta,
    )
    shared = lax.all_to_all(shared, "ga", split_axis=0, concat_axis=0, tiled=True)
    sent = pl.pallas_call(
        backward_kernel,
        out_shape=jax.ShapeDtypeStruct((N_GA, 40, COLS), f32),
        in_specs=[whole(pltpu.SMEM)] * 2 + [whole()] * 6 + [whole(pl.ANY)] * 2,
        out_specs=whole(),
        scratch_shapes=[
            pltpu.VMEM((row_count, 128), f32),
            pltpu.VMEM((HALF * PITCH, 128), f32),
            pltpu.VMEM((HALF * N, 128), f32),
            pltpu.VMEM((NCOL, 128), f32),
            pltpu.VMEM((SLOTS * 40, 128), f32),
            pltpu.VMEM((SLOTS, 128), f32),
            pltpu.SemaphoreType.DMA((2,)),
        ],
        compiler_params=pltpu.CompilerParams(vmem_limit_bytes=LIMIT),
        name="planes_backward",
    )(
        (site_y // 2) * N + site_x,
        box_base,
        shared,
        strength.reshape(1, ATOMS),
        box_atom.reshape(1, SLOTS),
        jnp.asarray(stage_matrix(-1.0, False)),
        jnp.asarray(stage_matrix(-1.0, True)),
        (site_y % 2).reshape(NCOL // 128, 128),
        applied,
        beta,
    )
    returned = lax.all_to_all(sent, "ga", split_axis=0, concat_axis=0, tiled=True)
    own = lax.dynamic_slice_in_dim(column_sites, lax.axis_index("ga") * COLS, COLS)
    plane_kinetic = (2.0 / float(N * N)) * (frequency(own // N) ** 2 + frequency(own % N) ** 2)
    result, gram = pl.pallas_call(
        finish_kernel,
        out_shape=(
            jax.ShapeDtypeStruct((2 * N, COLS), f32),
            jax.ShapeDtypeStruct((8, 2 * bands), f32),
        ),
        in_specs=[whole()] * 4 + [whole(pl.ANY)],
        out_specs=(whole(), whole()),
        scratch_shapes=[
            pltpu.VMEM((bands, 2 * N, COLS), f32),
            pltpu.VMEM((2 * bands, 128), f32),
            pltpu.SemaphoreType.DMA((bands // 2,)),
        ],
        compiler_params=pltpu.CompilerParams(vmem_limit_bytes=LIMIT),
        name="finish",
    )(
        jnp.asarray(backward_depth),
        returned.reshape(2 * N, COLS),
        trial,
        plane_kinetic.reshape(1, COLS),
        basis_all,
    )
    gram = lax.all_to_all(gram, "ga", split_axis=0, concat_axis=0, tiled=True)
    gram = (jnp.sum(gram, axis=0) * (1.0 / math.sqrt(N * NCOL))).reshape(bands, 2).T
    return (result.reshape(trial_bands.shape), gram[:, :, None])


def solution(mesh):
    placed = (
        P("band", None, None, "ga"),
        P("band", None, None, "ga"),
        P(),
        P("ga", None, None),
        P("ga", None),
        P("ga"),
        P("ga", None),
        P(),
    )
    return jax.shard_map(
        on_device,
        mesh=mesh,
        in_specs=placed,
        out_specs=(P("band", None, None, "ga"), P(None, None, "band")),
        check_vma=False,
    )
```

```python
import math

import jax
import jax.numpy as jnp
import numpy as np
from jax import lax
from jax.experimental import pallas as pl
from jax.experimental.pallas import tpu as pltpu
from jax.sharding import PartitionSpec as P

N = 160
HALF = N // 2
N_GA = 8
PLANES = N // N_GA
NCOL = 5120
COLS = NCOL // N_GA
SLOTS = 192
ROWS_X = N + 8
ATOMS = 1024
GROUP = 40
PITCH = 164
LIMIT = 60 * 1024 * 1024
bf16 = jnp.bfloat16
f32 = jnp.float32


def split_np(matrix):
    high = np.asarray(matrix, np.float32).astype(jnp.bfloat16)
    low = (np.asarray(matrix, np.float64) - high.astype(np.float64)).astype(np.float32).astype(jnp.bfloat16)
    return high, low


def fourier(orient):
    index = np.arange(N)
    angle = (np.outer(index, index) % N) * (2.0 * np.pi / N)
    return np.cos(angle), orient * np.sin(angle)


def stage_matrix(orient, paired):
    cosine, sine = fourier(orient)
    if paired:
        order = np.concatenate([np.arange(0, N, 2), np.arange(1, N, 2)])
        cosine, sine = cosine[:, order], sine[:, order]
    ch, cl = split_np(cosine)
    sh, sl = split_np(sine)
    return np.concatenate([ch, sh, ch, sh, cl, sl], axis=1)


def sent_order():
    rows = []
    for d in range(N_GA):
        for part, span in ((0, range(16)), (1, range(16)), (0, range(16, 20)), (1, range(16, 20))):
            rows += [(part, d * PLANES + p) for p in span]
    return rows


def depth_matrices():
    cosine, sine = fourier(1.0)
    full = np.block([[cosine, -sine], [sine, cosine]])
    back = np.block([[cosine, sine], [-sine, cosine]]) / float(N**3)
    order = np.array([part * N + z for part, z in sent_order()])
    tables = []
    for matrix in (full[order], back[:, order]):
        high, low = split_np(matrix)
        tables.append(np.concatenate([high, high, low], axis=1))
    return tables


def lanes():
    return lax.broadcasted_iota(jnp.int32, (1, 128), 1)


def fourier_rows(matrix, blocks):
    lane = lanes()
    sign = jnp.where(lane < 64, -1.0, 1.0).astype(f32)
    pieces = []
    for block in blocks:
        turned = pltpu.roll(block, 64, 1) * sign
        high = block.astype(bf16)
        low = (block - high.astype(f32)).astype(bf16)
        turned_high = turned.astype(bf16)
        turned_low = (turned - turned_high.astype(f32)).astype(bf16)
        pieces.append(jnp.concatenate([high, turned_high, low, turned_low, high, turned_high], axis=0))
    right = pieces[0] if len(pieces) == 1 else jnp.concatenate(pieces, axis=1)
    return jnp.dot(matrix, right, preferred_element_type=f32)


def exchange_pairs(first, second):
    odd = (lanes() // 32) % 2 == 1
    even_rows = jnp.where(odd, pltpu.roll(second, 32, 1), first)
    odd_rows = jnp.where(odd, second, pltpu.roll(first, 96, 1))
    return jnp.concatenate([even_rows, odd_rows], axis=0)


def split3(values):
    high = values.astype(bf16)
    rest = values - high.astype(f32)
    middle = rest.astype(bf16)
    return high, middle, (rest - middle.astype(f32)).astype(bf16)


def exact_dot(first, second, contract):
    total = None
    if isinstance(first, tuple):
        terms = [(piece, second) for piece in first]
    else:
        terms = [(first, piece) for piece in second]
    for left, right in terms:
        product = lax.dot_general(left, right, (contract, ((), ())), preferred_element_type=f32)
        total = product if total is None else total + product
    return total


def atom_table(atoms):
    row = lax.broadcasted_iota(jnp.int32, (ATOMS, SLOTS), 0)
    return jnp.where(atoms[...] == row, 1.0, 0.0).astype(bf16)


def box_places(box_base, s):
    places = []
    for i in range(5):
        start = box_base[s] + i * ROWS_X
        places.append(pl.ds(jnp.where(start >= HALF * ROWS_X, start - HALF * ROWS_X, start), 8))
    return places


def depth_product(matrix, values):
    high = values.astype(bf16)
    low = (values - high.astype(f32)).astype(bf16)
    return jnp.dot(matrix, jnp.concatenate([high, low, high], axis=0), preferred_element_type=f32)


def depth_kernel(matrix, values, out):
    out[...] = depth_product(matrix[...], values[...])


def prepare_kernel(
    box_plane, box_odd, potential, box_beta, potential_out, beta_out, rows, table, sems
):
    copies = []

    def send(source, target, start, size):
        span = pl.ds(start, size)
        copies.append(pltpu.make_async_copy(source.at[span], target.at[span], sems.at[len(copies)]))
        copies[-1].start()

    lane = lanes()
    lane_odd = (lane // 32) % 2 == 1
    lane_plane = lane % 32
    local_box = lax.broadcasted_iota(jnp.int32, (16, 128), 0) % 8
    local_plane = lane_plane - lax.broadcasted_iota(jnp.int32, (16, 128), 0) // 8
    nothing = jnp.zeros((8, 128), f32)

    def spread(t, carry):
        values = box_beta[pl.ds(pl.multiple_of(t * 8, 8), 8), :]
        both = jnp.concatenate([values, pltpu.roll(values, 64, 1)], axis=0)
        high = both.astype(bf16).astype(f32)
        left = jnp.concatenate([high, both - high], axis=0).T[0:64].astype(bf16)
        masks = []
        for k in range(8):
            hit = (local_box == k) & (local_plane == box_plane[t * 8 + k])
            masks.append(jnp.where(hit, 1.0, 0.0))
        mask = jnp.concatenate(masks, axis=1)
        right = jnp.concatenate([mask, mask], axis=0).astype(bf16)
        lines = jnp.dot(left, right, preferred_element_type=f32)
        for k in range(8):
            s = t * 8 + k
            shifted = box_odd[s] > 0
            line = [lines[x * 8 : x * 8 + 8, k * 128 : (k + 1) * 128] for x in range(8)]
            for i in range(5):
                even = line[2 * i] if i < 4 else nothing
                straight = jnp.where(lane_odd, line[2 * i + 1], even) if i < 4 else nothing
                moved = jnp.where(lane_odd, even, line[2 * i - 1] if i > 0 else nothing)
                table[pl.ds(pl.multiple_of(s * 40 + i * 8, 8), 8), :] = jnp.where(shifted, moved, straight)
        return carry

    def spread_two(t, carry):
        spread(2 * t, 0)
        spread(2 * t + 1, 0)
        return carry

    for piece in range(2):
        lax.fori_loop(piece * 6, piece * 6 + 6, spread_two, 0)
        send(table, beta_out, piece * SLOTS * 20, SLOTS * 20)
    zero = jnp.zeros((8, N), f32)
    for piece in range(4):
        for k in range(HALF // 4):
            pair = piece * (HALF // 4) + k
            pieces = []
            for half in range(2):
                plane = potential[:, 2 * pair + half, :]
                pieces += [plane[0:8], plane[8:16], jnp.concatenate([plane[16:20], zero[0:4]], axis=0), zero]
            stacked = jnp.concatenate(pieces + pieces, axis=0)
            rows[pair * N : pair * N + 128, :] = stacked[:, 0:128].T
            rows[pair * N + 128 : pair * N + N, :] = stacked[:, 128:N].T
        send(rows, potential_out, piece * (HALF // 4) * N, (HALF // 4) * N)
    for copy in copies:
        copy.wait()


def finish_kernel(core, matrix, returned, trial, plane_kinetic, result, away):
    depth = lax.broadcasted_iota(jnp.int32, (N, 1), 0)
    depth = jnp.where(depth < HALF, depth, depth - N).astype(f32)
    kinetic = (2.0 / float(N * N)) * (depth * depth) + plane_kinetic[...]
    spectrum = depth_product(matrix[...], returned[...])
    first = core[0] == 0
    for part in range(2):
        rows = slice(part * N, part * N + N)
        values = spectrum[rows] + kinetic * trial[rows, :]
        result[rows, :] = values
        away[part * HALF : part * HALF + HALF, :] = jnp.where(first, values[HALF:N], values[0:HALF])


def gram_kernel(core, result, brought, basis_all, gram, basis, own_sums, other_sums, sems):
    chips = basis_all.shape[0]

    def fetch(m):
        return pltpu.make_async_copy(basis_all.at[m], basis.at[m], sems.at[m])

    for m in range(chips):
        fetch(m).start()
    half = core[0] * HALF

    def one_chip(m, carry):
        fetch(m).wait()
        chip = jnp.where(m < chips // 2, 2 * m, 2 * chips - 1 - 2 * m)

        def rows(t, totals):
            totals = list(totals)
            row = pl.multiple_of(t * 8, 8)
            here = (pl.ds(row, 8), pl.ds(row + HALF, 8))
            mine = (pl.ds(pl.multiple_of(half + row, 8), 8), pl.ds(pl.multiple_of(half + N + row, 8), 8))
            for j in range(COLS // 128):
                tile = slice(j * 128, (j + 1) * 128)
                rights = [(result[mine[0], tile], result[mine[1], tile]), (brought[here[0], tile], brought[here[1], tile])]
                for slot in range(2):
                    left_real, left_imag = basis[m, slot, here[0], tile], basis[m, slot, here[1], tile]
                    for n, (real, imag) in enumerate(rights):
                        at = n * 4 + slot * 2
                        totals[at] = totals[at] + (left_real * real + left_imag * imag)
                        totals[at + 1] = totals[at + 1] + (left_real * imag - left_imag * real)
            return tuple(totals)

        totals = lax.fori_loop(0, HALF // 8, rows, (jnp.zeros((8, 128), f32),) * 8)
        for at in range(4):
            own_sums[pl.ds(chip * 4 + at, 1), :] = jnp.sum(totals[at], axis=0, keepdims=True)
            other_sums[pl.ds(chip * 4 + at, 1), :] = jnp.sum(totals[4 + at], axis=0, keepdims=True)
        return carry

    lax.fori_loop(0, chips, one_chip, 0)
    ones = jnp.ones((8, 128), bf16)
    own = exact_dot(ones, split3(own_sums[...]), ((1,), (1,)))
    other = exact_dot(ones, split3(other_sums[...]), ((1,), (1,)))
    first = core[0] == 0
    gram[0:8, :] = jnp.where(first, own, other)
    gram[8:16, :] = jnp.where(first, other, own)


def forward_kernel(
    site_row, box_base, recv, first_matrix, second_matrix, atoms, potential_in, beta_in,
    applied_out, shared, grid, mixed, stage, sums, applied, potential, beta, sems,
):
    potential_copy = pltpu.make_async_copy(potential_in, potential, sems.at[0])
    beta_copy = pltpu.make_async_copy(beta_in, beta, sems.at[1])
    potential_copy.start()
    beta_copy.start()

    def transpose(d, carry):
        for j in range(COLS // 128):
            block = recv[d, :, j * 128 : (j + 1) * 128]
            real, imag, rest = block[0:16], block[16:32], block[32:40]
            swapped = pltpu.roll(rest, 4, 0)
            zero = jnp.zeros((8, 128), f32)
            stacked = jnp.concatenate(
                [real, rest, zero, real, rest, zero, imag, swapped, zero, imag, swapped, zero], axis=0
            )
            stage[pl.ds(pl.multiple_of(d * COLS + j * 128, 128), 128), :] = stacked.T
        return carry

    lax.fori_loop(0, N_GA, transpose, 0)

    def clear(t, carry):
        grid[pl.ds(pl.multiple_of(t * 256, 256), 256), :] = jnp.zeros((256, 128), f32)
        return carry

    lax.fori_loop(0, N * N // 256, clear, 0)

    def place(t, carry):
        base = t * 64
        for k in range(64):
            grid[pl.ds(site_row[base + k], 1), :] = stage[pl.ds(base + k, 1), :]
        return carry

    lax.fori_loop(0, NCOL // 64, place, 0)

    odd = (lanes() // 32) % 2 == 1

    def along_x(t, carry):
        blocks = []
        for k in range(GROUP):
            start = pl.multiple_of((t * GROUP + k) * 2 * N, 16)
            even_y = grid[pl.ds(start, N), :]
            odd_y = grid[pl.ds(start + N, N), :]
            blocks.append(jnp.where(odd, odd_y, even_y))
        result = fourier_rows(first_matrix[...], blocks)
        for k in range(GROUP):
            mixed[pl.ds((t * GROUP + k) * PITCH, N), :] = result[:, k * 128 : (k + 1) * 128]
        return carry

    lax.fori_loop(0, HALF // GROUP, along_x, 0)
    potential_copy.wait()

    def along_y(t, carry):
        blocks = []
        for k in range(GROUP):
            pair = t * GROUP + k
            blocks.append(
                exchange_pairs(
                    mixed[pl.ds(2 * pair, HALF, stride=PITCH), :], mixed[pl.ds(2 * pair + 1, HALF, stride=PITCH), :]
                )
            )
        result = fourier_rows(second_matrix[...], blocks)
        for k in range(GROUP):
            pair = t * GROUP + k
            values = result[:, k * 128 : (k + 1) * 128]
            start = pl.multiple_of(pair * ROWS_X, 8)
            grid[pl.ds(start, N), :] = values
            grid[pl.ds(start + N, 8), :] = values[0:8]
            applied[pl.ds(start, N), :] = values * potential[pl.ds(pl.multiple_of(pair * N, 16), N), :]
            applied[pl.ds(start + N, 8), :] = jnp.zeros((8, 128), f32)
        return carry

    copies = []
    for t in range(HALF // GROUP):
        along_y(t, 0)
        piece = pl.ds(t * GROUP * ROWS_X, GROUP * ROWS_X)
        copy = pltpu.make_async_copy(applied.at[piece], applied_out.at[piece], sems.at[2 + t])
        copy.start()
        copies.append(copy)
    beta_copy.wait()

    def project(t, carry):
        for k in range(4):
            s = t * 4 + k
            total = jnp.zeros((8, 128), f32)
            for i, place in enumerate(box_places(box_base, s)):
                weight = beta[pl.ds(pl.multiple_of(s * 40 + i * 8, 8), 8), :]
                total = total + weight * grid[place, :]
            sums[pl.ds(pl.multiple_of(s * 8, 8), 8), :] = total
        return carry

    lax.fori_loop(0, SLOTS // 4, project, 0)
    totals = jnp.sum(sums[...].reshape(SLOTS, 8, 128), axis=1)
    row = lax.broadcasted_iota(jnp.int32, (8, 128), 0)
    column = lax.broadcasted_iota(jnp.int32, (8, 128), 1)
    chooser = jnp.where(row == column // 64, 1.0, 0.0).astype(bf16)
    partial = exact_dot(chooser, split3(totals), ((1,), (1,)))
    by_atom = exact_dot(split3(partial), atom_table(atoms), ((1,), (1,)))
    for part in range(2):
        for r in range(4):
            values = by_atom[part : part + 1, r * 256 : (r + 1) * 256]
            for d in range(N_GA):
                shared[d, part * 4 + r : part * 4 + r + 1, :] = values
    for copy in copies:
        copy.wait()


def backward_kernel(
    site_row, box_base, shared, strength, atoms, first_matrix, second_matrix, parity, applied_in, beta_in,
    sent, applied, mixed, grid, stage, beta, weights, sems,
):
    applied_copy = pltpu.make_async_copy(applied_in, applied, sems.at[0])
    beta_copy = pltpu.make_async_copy(beta_in, beta, sems.at[1])
    applied_copy.start()
    beta_copy.start()
    total = jnp.sum(shared[...], axis=0)
    by_part = []
    for part in range(2):
        whole_row = jnp.concatenate([total[part * 4 + r : part * 4 + r + 1, :] for r in range(4)], axis=1)
        by_part.append(jnp.broadcast_to(whole_row * strength[...], (64, ATOMS)))
    spread = jnp.concatenate(by_part, axis=0)
    weights[...] = exact_dot(split3(spread), atom_table(atoms), ((1,), (0,))).T
    applied_copy.wait()
    beta_copy.wait()

    def add_boxes(t, carry):
        for k in range(2):
            s = t * 2 + k
            weight = weights[pl.ds(s, 1), :]
            places = box_places(box_base, s)
            olds = [applied[place, :] for place in places]
            for i in range(5):
                applied[places[i], :] = olds[i] + beta[pl.ds(pl.multiple_of(s * 40 + i * 8, 8), 8), :] * weight
        return carry

    lax.fori_loop(0, SLOTS // 2, add_boxes, 0)

    def along_y(t, carry):
        blocks = []
        for k in range(GROUP):
            start = pl.multiple_of((t * GROUP + k) * ROWS_X, 8)
            top = applied[pl.ds(start, 8), :] + applied[pl.ds(start + N, 8), :]
            blocks.append(jnp.concatenate([top, applied[pl.ds(start + 8, N - 8), :]], axis=0))
        result = fourier_rows(first_matrix[...], blocks)
        for k in range(GROUP):
            mixed[pl.ds((t * GROUP + k) * PITCH, N), :] = result[:, k * 128 : (k + 1) * 128]
        return carry

    lax.fori_loop(0, HALF // GROUP, along_y, 0)

    def along_x(t, carry):
        blocks = []
        for k in range(GROUP):
            pair = t * GROUP + k
            blocks.append(
                exchange_pairs(
                    mixed[pl.ds(2 * pair, HALF, stride=PITCH), :], mixed[pl.ds(2 * pair + 1, HALF, stride=PITCH), :]
                )
            )
        result = fourier_rows(second_matrix[...], blocks)
        for k in range(GROUP):
            grid[pl.ds(pl.multiple_of((t * GROUP + k) * N, 16), N), :] = result[:, k * 128 : (k + 1) * 128]
        return carry

    lax.fori_loop(0, HALF // GROUP, along_x, 0)

    def pick(t, carry):
        base = t * 64
        for k in range(64):
            stage[pl.ds(base + k, 1), :] = grid[pl.ds(site_row[base + k], 1), :]
        return carry

    lax.fori_loop(0, NCOL // 64, pick, 0)
    upper = lax.broadcasted_iota(jnp.int32, (8, 128), 0) < 4

    def transpose(d, carry):
        for j in range(COLS // 128):
            turned = stage[pl.ds(pl.multiple_of(d * COLS + j * 128, 128), 128), :].T
            is_odd = parity[pl.ds(d * (COLS // 128) + j, 1), :] > 0
            real = jnp.where(is_odd, turned[32:56], turned[0:24])
            imag = jnp.where(is_odd, turned[96:120], turned[64:88])
            rest = jnp.where(upper, real[16:24], pltpu.roll(imag[16:24], 4, 0))
            sent[d, :, j * 128 : (j + 1) * 128] = jnp.concatenate([real[0:16], imag[0:16], rest], axis=0)
        return carry

    lax.fori_loop(0, N_GA, transpose, 0)


def whole(space=pltpu.VMEM):
    return pl.BlockSpec(memory_space=space)


def frequency(index):
    return jnp.where(index < HALF, index, index - N).astype(f32)


def on_device(trial_bands, basis_bands, column_sites, potential, box_cells, box_atom, box_beta, strength):
    forward_depth, backward_depth = depth_matrices()
    bands = lax.axis_size("band")
    core = lax.axis_index("band") % 2
    halves = basis_bands.reshape(2, 2, HALF, COLS)
    swap = [(i, i ^ 1) for i in range(bands)]
    kept = jnp.where(core == 0, halves[:, 0], halves[:, 1])
    given = jnp.where(core == 0, halves[:, 1], halves[:, 0])
    taken = lax.ppermute(given, "band", swap)
    block = jnp.where(core == 0, jnp.stack([kept, taken]), jnp.stack([taken, kept])).reshape(2, N, COLS)
    chip_order = list(range(0, bands // 2, 2)) + list(range(bands // 2 - 1, 0, -2))
    rings = [[2 * chip + k for chip in chip_order] for k in range(2)]
    basis_all = lax.all_gather(block, "band", axis=0, axis_index_groups=rings)
    trial = trial_bands.reshape(2 * N, COLS)
    depth = pl.pallas_call(
        depth_kernel,
        out_shape=jax.ShapeDtypeStruct((2 * N, COLS), f32),
        in_specs=[whole()] * 2,
        out_specs=whole(),
        compiler_params=pltpu.CompilerParams(vmem_limit_bytes=LIMIT),
        name="depth",
    )(jnp.asarray(forward_depth), trial)
    recv = lax.all_to_all(depth.reshape(N_GA, 40, COLS), "ga", split_axis=0, concat_axis=0, tiled=True)

    site_x = column_sites // N
    site_y = column_sites - site_x * N
    corner = box_cells[:, 0]
    corner_plane = corner // (N * N)
    in_plane = corner - corner_plane * (N * N)
    corner_x = in_plane // N
    box_base = (corner_x // 2) * ROWS_X + (in_plane - corner_x * N)
    pot, beta = pl.pallas_call(
        prepare_kernel,
        out_shape=(
            jax.ShapeDtypeStruct((HALF * N, 128), f32),
            jax.ShapeDtypeStruct((SLOTS * 40, 128), f32),
        ),
        in_specs=[whole(pltpu.SMEM)] * 2 + [whole()] * 2,
        out_specs=(whole(pl.ANY), whole(pl.ANY)),
        scratch_shapes=[
            pltpu.VMEM((HALF * N, 128), f32),
            pltpu.VMEM((SLOTS * 40, 128), f32),
            pltpu.SemaphoreType.DMA((6,)),
        ],
        compiler_params=pltpu.CompilerParams(vmem_limit_bytes=LIMIT),
        cost_estimate=pl.CostEstimate(flops=0, bytes_accessed=14000000, transcendentals=0),
        name="prepare",
    )(corner_plane, corner_x % 2, potential, box_beta)
    row_count = HALF * ROWS_X
    applied, shared = pl.pallas_call(
        forward_kernel,
        out_shape=(
            jax.ShapeDtypeStruct((row_count, 128), f32),
            jax.ShapeDtypeStruct((N_GA, 8, ATOMS // 4), f32),
        ),
        in_specs=[whole(pltpu.SMEM)] * 2 + [whole()] * 4 + [whole(pl.ANY)] * 2,
        out_specs=(whole(pl.ANY), whole()),
        scratch_shapes=[
            pltpu.VMEM((N * N, 128), f32),
            pltpu.VMEM((HALF * PITCH, 128), f32),
            pltpu.VMEM((NCOL, 128), f32),
            pltpu.VMEM((SLOTS * 8, 128), f32),
            pltpu.VMEM((row_count, 128), f32),
            pltpu.VMEM((HALF * N, 128), f32),
            pltpu.VMEM((SLOTS * 40, 128), f32),
            pltpu.SemaphoreType.DMA((2 + HALF // GROUP,)),
        ],
        compiler_params=pltpu.CompilerParams(vmem_limit_bytes=LIMIT),
        name="planes_forward",
    )(
        site_y * N + site_x,
        box_base,
        recv,
        jnp.asarray(stage_matrix(1.0, False)),
        jnp.asarray(stage_matrix(1.0, True)),
        box_atom.reshape(1, SLOTS),
        pot,
        beta,
    )
    shared = lax.all_to_all(shared, "ga", split_axis=0, concat_axis=0, tiled=True)
    sent = pl.pallas_call(
        backward_kernel,
        out_shape=jax.ShapeDtypeStruct((N_GA, 40, COLS), f32),
        in_specs=[whole(pltpu.SMEM)] * 2 + [whole()] * 6 + [whole(pl.ANY)] * 2,
        out_specs=whole(),
        scratch_shapes=[
            pltpu.VMEM((row_count, 128), f32),
            pltpu.VMEM((HALF * PITCH, 128), f32),
            pltpu.VMEM((HALF * N, 128), f32),
            pltpu.VMEM((NCOL, 128), f32),
            pltpu.VMEM((SLOTS * 40, 128), f32),
            pltpu.VMEM((SLOTS, 128), f32),
            pltpu.SemaphoreType.DMA((2,)),
        ],
        compiler_params=pltpu.CompilerParams(vmem_limit_bytes=LIMIT),
        name="planes_backward",
    )(
        (site_y // 2) * N + site_x,
        box_base,
        shared,
        strength.reshape(1, ATOMS),
        box_atom.reshape(1, SLOTS),
        jnp.asarray(stage_matrix(-1.0, False)),
        jnp.asarray(stage_matrix(-1.0, True)),
        (site_y % 2).reshape(NCOL // 128, 128),
        applied,
        beta,
    )
    returned = lax.all_to_all(sent, "ga", split_axis=0, concat_axis=0, tiled=True)
    own = lax.dynamic_slice_in_dim(column_sites, lax.axis_index("ga") * COLS, COLS)
    plane_kinetic = (2.0 / float(N * N)) * (frequency(own // N) ** 2 + frequency(own % N) ** 2)
    core_number = core.reshape(1)
    result, away = pl.pallas_call(
        finish_kernel,
        out_shape=(jax.ShapeDtypeStruct((2 * N, COLS), f32), jax.ShapeDtypeStruct((N, COLS), f32)),
        in_specs=[whole(pltpu.SMEM)] + [whole()] * 4,
        out_specs=(whole(), whole()),
        compiler_params=pltpu.CompilerParams(vmem_limit_bytes=LIMIT),
        name="finish",
    )(
        core_number,
        jnp.asarray(backward_depth),
        returned.reshape(2 * N, COLS),
        trial,
        plane_kinetic.reshape(1, COLS),
    )
    brought = lax.ppermute(away, "band", swap)
    gram = pl.pallas_call(
        gram_kernel,
        out_shape=jax.ShapeDtypeStruct((16, 2 * bands), f32),
        in_specs=[whole(pltpu.SMEM)] + [whole()] * 2 + [whole(pl.ANY)],
        out_specs=whole(),
        scratch_shapes=[
            pltpu.VMEM((bands // 2, 2, N, COLS), f32),
            pltpu.VMEM((2 * bands, 128), f32),
            pltpu.VMEM((2 * bands, 128), f32),
            pltpu.SemaphoreType.DMA((bands // 2,)),
        ],
        compiler_params=pltpu.CompilerParams(vmem_limit_bytes=LIMIT),
        name="gram",
    )(core_number, result, brought, basis_all)
    chip_group = [[(2 * chip + k) * N_GA + g for k in range(2) for g in range(N_GA)] for chip in range(bands // 2)]
    gram = lax.all_to_all(
        gram, ("band", "ga"), split_axis=0, concat_axis=0, tiled=True, axis_index_groups=chip_group
    )
    gram = (jnp.sum(gram, axis=0) * (1.0 / math.sqrt(N * NCOL))).reshape(bands, 2).T
    return (result.reshape(trial_bands.shape), gram[:, :, None])


def solution(mesh):
    placed = (
        P("band", None, None, "ga"),
        P("band", None, None, "ga"),
        P(),
        P("ga", None, None),
        P("ga", None),
        P("ga"),
        P("ga", None),
        P(),
    )
    return jax.shard_map(
        on_device,
        mesh=mesh,
        in_specs=placed,
        out_specs=(P("band", None, None, "ga"), P(None, None, "band")),
        check_vma=False,
    )
```

```python
import math

import jax
import jax.numpy as jnp
import numpy as np
from jax import lax
from jax.experimental import pallas as pl
from jax.experimental.pallas import tpu as pltpu
from jax.sharding import PartitionSpec as P

N = 160
HALF = N // 2
N_GA = 8
PLANES = N // N_GA
NCOL = 5120
COLS = NCOL // N_GA
SLOTS = 192
ROWS_X = N + 8
ATOMS = 1024
GROUP = 40
PITCH = 164
LIMIT = 60 * 1024 * 1024
KEPT = 8 * 1024 * 1024
bf16 = jnp.bfloat16
f32 = jnp.float32


def split_np(matrix):
    high = np.asarray(matrix, np.float32).astype(jnp.bfloat16)
    low = (np.asarray(matrix, np.float64) - high.astype(np.float64)).astype(np.float32).astype(jnp.bfloat16)
    return high, low


def fourier(orient):
    index = np.arange(N)
    angle = (np.outer(index, index) % N) * (2.0 * np.pi / N)
    return np.cos(angle), orient * np.sin(angle)


def stage_matrix(orient, paired):
    cosine, sine = fourier(orient)
    if paired:
        order = np.concatenate([np.arange(0, N, 2), np.arange(1, N, 2)])
        cosine, sine = cosine[:, order], sine[:, order]
    ch, cl = split_np(cosine)
    sh, sl = split_np(sine)
    return np.concatenate([ch, sh, ch, sh, cl, sl], axis=1)


def sent_order():
    rows = []
    for d in range(N_GA):
        for part, span in ((0, range(16)), (1, range(16)), (0, range(16, 20)), (1, range(16, 20))):
            rows += [(part, d * PLANES + p) for p in span]
    return rows


def depth_matrices():
    cosine, sine = fourier(1.0)
    full = np.block([[cosine, -sine], [sine, cosine]])
    back = np.block([[cosine, sine], [-sine, cosine]]) / float(N**3)
    order = np.array([part * N + z for part, z in sent_order()])
    tables = []
    for matrix in (full[order], back[:, order]):
        high, low = split_np(matrix)
        tables.append(np.concatenate([high, high, low], axis=1))
    return tables


def lanes():
    return lax.broadcasted_iota(jnp.int32, (1, 128), 1)


def fourier_rows(matrix, blocks):
    lane = lanes()
    sign = jnp.where(lane < 64, -1.0, 1.0).astype(f32)
    pieces = []
    for block in blocks:
        turned = pltpu.roll(block, 64, 1) * sign
        high = block.astype(bf16)
        low = (block - high.astype(f32)).astype(bf16)
        turned_high = turned.astype(bf16)
        turned_low = (turned - turned_high.astype(f32)).astype(bf16)
        pieces.append(jnp.concatenate([high, turned_high, low, turned_low, high, turned_high], axis=0))
    right = pieces[0] if len(pieces) == 1 else jnp.concatenate(pieces, axis=1)
    return jnp.dot(matrix, right, preferred_element_type=f32)


def exchange_pairs(first, second):
    odd = (lanes() // 32) % 2 == 1
    even_rows = jnp.where(odd, pltpu.roll(second, 32, 1), first)
    odd_rows = jnp.where(odd, second, pltpu.roll(first, 96, 1))
    return jnp.concatenate([even_rows, odd_rows], axis=0)


def split3(values):
    high = values.astype(bf16)
    rest = values - high.astype(f32)
    middle = rest.astype(bf16)
    return high, middle, (rest - middle.astype(f32)).astype(bf16)


def exact_dot(first, second, contract):
    total = None
    if isinstance(first, tuple):
        terms = [(piece, second) for piece in first]
    else:
        terms = [(first, piece) for piece in second]
    for left, right in terms:
        product = lax.dot_general(left, right, (contract, ((), ())), preferred_element_type=f32)
        total = product if total is None else total + product
    return total


def atom_table(atoms):
    row = lax.broadcasted_iota(jnp.int32, (ATOMS, SLOTS), 0)
    return jnp.where(atoms[...] == row, 1.0, 0.0).astype(bf16)


def box_places(box_base, s):
    places = []
    for i in range(5):
        start = box_base[s] + i * ROWS_X
        places.append(pl.ds(jnp.where(start >= HALF * ROWS_X, start - HALF * ROWS_X, start), 8))
    return places


def depth_product(matrix, values):
    high = values.astype(bf16)
    low = (values - high.astype(f32)).astype(bf16)
    return jnp.dot(matrix, jnp.concatenate([high, low, high], axis=0), preferred_element_type=f32)


def depth_kernel(matrix, values, out):
    out[...] = depth_product(matrix[...], values[...])


def prepare_kernel(
    box_plane, box_odd, potential, box_beta, potential_out, beta_out, rows, table, sems
):
    copies = []

    def send(source, target, start, size):
        span = pl.ds(start, size)
        copies.append(pltpu.make_async_copy(source.at[span], target.at[span], sems.at[len(copies)]))
        copies[-1].start()

    lane = lanes()
    lane_odd = (lane // 32) % 2 == 1
    lane_plane = lane % 32
    local_box = lax.broadcasted_iota(jnp.int32, (16, 128), 0) % 8
    local_plane = lane_plane - lax.broadcasted_iota(jnp.int32, (16, 128), 0) // 8
    nothing = jnp.zeros((8, 128), f32)

    def spread(t, carry):
        values = box_beta[pl.ds(pl.multiple_of(t * 8, 8), 8), :]
        both = jnp.concatenate([values, pltpu.roll(values, 64, 1)], axis=0)
        high = both.astype(bf16).astype(f32)
        left = jnp.concatenate([high, both - high], axis=0).T[0:64].astype(bf16)
        masks = []
        for k in range(8):
            hit = (local_box == k) & (local_plane == box_plane[t * 8 + k])
            masks.append(jnp.where(hit, 1.0, 0.0))
        mask = jnp.concatenate(masks, axis=1)
        right = jnp.concatenate([mask, mask], axis=0).astype(bf16)
        lines = jnp.dot(left, right, preferred_element_type=f32)
        for k in range(8):
            s = t * 8 + k
            shifted = box_odd[s] > 0
            line = [lines[x * 8 : x * 8 + 8, k * 128 : (k + 1) * 128] for x in range(8)]
            for i in range(5):
                even = line[2 * i] if i < 4 else nothing
                straight = jnp.where(lane_odd, line[2 * i + 1], even) if i < 4 else nothing
                moved = jnp.where(lane_odd, even, line[2 * i - 1] if i > 0 else nothing)
                table[pl.ds(pl.multiple_of(s * 40 + i * 8, 8), 8), :] = jnp.where(shifted, moved, straight)
        return carry

    def spread_two(t, carry):
        spread(2 * t, 0)
        spread(2 * t + 1, 0)
        return carry

    for piece in range(2):
        lax.fori_loop(piece * 6, piece * 6 + 6, spread_two, 0)
        send(table, beta_out, piece * SLOTS * 20, SLOTS * 20)
    zero = jnp.zeros((8, N), f32)
    for piece in range(4):
        for k in range(HALF // 4):
            pair = piece * (HALF // 4) + k
            pieces = []
            for half in range(2):
                plane = potential[:, 2 * pair + half, :]
                pieces += [plane[0:8], plane[8:16], jnp.concatenate([plane[16:20], zero[0:4]], axis=0), zero]
            stacked = jnp.concatenate(pieces + pieces, axis=0)
            rows[pair * N : pair * N + 128, :] = stacked[:, 0:128].T
            rows[pair * N + 128 : pair * N + N, :] = stacked[:, 128:N].T
        send(rows, potential_out, piece * (HALF // 4) * N, (HALF // 4) * N)
    for copy in copies:
        copy.wait()


def finish_kernel(core, matrix, returned, trial, plane_kinetic, result, away):
    depth = lax.broadcasted_iota(jnp.int32, (N, 1), 0)
    depth = jnp.where(depth < HALF, depth, depth - N).astype(f32)
    kinetic = (2.0 / float(N * N)) * (depth * depth) + plane_kinetic[...]
    spectrum = depth_product(matrix[...], returned[...])
    first = core[0] == 0
    for part in range(2):
        rows = slice(part * N, part * N + N)
        values = spectrum[rows] + kinetic * trial[rows, :]
        result[rows, :] = values
        away[part * HALF : part * HALF + HALF, :] = jnp.where(first, values[HALF:N], values[0:HALF])


def gram_kernel(core, result, brought, basis_all, gram, basis, own_sums, other_sums, sems):
    chips = basis_all.shape[0]

    def fetch(m):
        return pltpu.make_async_copy(basis_all.at[m], basis.at[m], sems.at[m])

    for m in range(chips):
        fetch(m).start()
    half = core[0] * HALF

    def one_chip(m, carry):
        fetch(m).wait()
        chip = jnp.where(m < chips // 2, 2 * m, 2 * chips - 1 - 2 * m)

        def rows(t, totals):
            totals = list(totals)
            row = pl.multiple_of(t * 8, 8)
            here = (pl.ds(row, 8), pl.ds(row + HALF, 8))
            mine = (pl.ds(pl.multiple_of(half + row, 8), 8), pl.ds(pl.multiple_of(half + N + row, 8), 8))
            for j in range(COLS // 128):
                tile = slice(j * 128, (j + 1) * 128)
                rights = [(result[mine[0], tile], result[mine[1], tile]), (brought[here[0], tile], brought[here[1], tile])]
                for slot in range(2):
                    left_real, left_imag = basis[m, slot, here[0], tile], basis[m, slot, here[1], tile]
                    for n, (real, imag) in enumerate(rights):
                        at = n * 4 + slot * 2
                        totals[at] = totals[at] + (left_real * real + left_imag * imag)
                        totals[at + 1] = totals[at + 1] + (left_real * imag - left_imag * real)
            return tuple(totals)

        totals = lax.fori_loop(0, HALF // 8, rows, (jnp.zeros((8, 128), f32),) * 8)
        for at in range(4):
            own_sums[pl.ds(chip * 4 + at, 1), :] = jnp.sum(totals[at], axis=0, keepdims=True)
            other_sums[pl.ds(chip * 4 + at, 1), :] = jnp.sum(totals[4 + at], axis=0, keepdims=True)
        return carry

    lax.fori_loop(0, chips, one_chip, 0)
    ones = jnp.ones((8, 128), bf16)
    own = exact_dot(ones, split3(own_sums[...]), ((1,), (1,)))
    other = exact_dot(ones, split3(other_sums[...]), ((1,), (1,)))
    first = core[0] == 0
    gram[0:8, :] = jnp.where(first, own, other)
    gram[8:16, :] = jnp.where(first, other, own)


def forward_kernel(
    site_row, box_base, recv, first_matrix, second_matrix, atoms, potential_in, beta_in,
    applied, shared, grid, mixed, stage, sums, potential, beta, sems,
):
    potential_copy = pltpu.make_async_copy(potential_in, potential, sems.at[0])
    beta_copy = pltpu.make_async_copy(beta_in, beta, sems.at[1])
    potential_copy.start()
    beta_copy.start()

    def transpose(d, carry):
        for j in range(COLS // 128):
            block = recv[d, :, j * 128 : (j + 1) * 128]
            real, imag, rest = block[0:16], block[16:32], block[32:40]
            swapped = pltpu.roll(rest, 4, 0)
            zero = jnp.zeros((8, 128), f32)
            stacked = jnp.concatenate(
                [real, rest, zero, real, rest, zero, imag, swapped, zero, imag, swapped, zero], axis=0
            )
            stage[pl.ds(pl.multiple_of(d * COLS + j * 128, 128), 128), :] = stacked.T
        return carry

    lax.fori_loop(0, N_GA, transpose, 0)

    def clear(t, carry):
        grid[pl.ds(pl.multiple_of(t * 256, 256), 256), :] = jnp.zeros((256, 128), f32)
        return carry

    lax.fori_loop(0, N * N // 256, clear, 0)

    def place(t, carry):
        base = t * 64
        for k in range(64):
            grid[pl.ds(site_row[base + k], 1), :] = stage[pl.ds(base + k, 1), :]
        return carry

    lax.fori_loop(0, NCOL // 64, place, 0)

    odd = (lanes() // 32) % 2 == 1

    def along_x(t, carry):
        blocks = []
        for k in range(GROUP):
            start = pl.multiple_of((t * GROUP + k) * 2 * N, 16)
            even_y = grid[pl.ds(start, N), :]
            odd_y = grid[pl.ds(start + N, N), :]
            blocks.append(jnp.where(odd, odd_y, even_y))
        result = fourier_rows(first_matrix[...], blocks)
        for k in range(GROUP):
            mixed[pl.ds((t * GROUP + k) * PITCH, N), :] = result[:, k * 128 : (k + 1) * 128]
        return carry

    lax.fori_loop(0, HALF // GROUP, along_x, 0)
    potential_copy.wait()

    def along_y(t, carry):
        blocks = []
        for k in range(GROUP):
            pair = t * GROUP + k
            blocks.append(
                exchange_pairs(
                    mixed[pl.ds(2 * pair, HALF, stride=PITCH), :], mixed[pl.ds(2 * pair + 1, HALF, stride=PITCH), :]
                )
            )
        result = fourier_rows(second_matrix[...], blocks)
        for k in range(GROUP):
            pair = t * GROUP + k
            values = result[:, k * 128 : (k + 1) * 128]
            start = pl.multiple_of(pair * ROWS_X, 8)
            grid[pl.ds(start, N), :] = values
            grid[pl.ds(start + N, 8), :] = values[0:8]
            applied[pl.ds(start, N), :] = values * potential[pl.ds(pl.multiple_of(pair * N, 16), N), :]
            applied[pl.ds(start + N, 8), :] = jnp.zeros((8, 128), f32)
        return carry

    for t in range(HALF // GROUP):
        along_y(t, 0)
    beta_copy.wait()

    def project(t, carry):
        for k in range(4):
            s = t * 4 + k
            total = jnp.zeros((8, 128), f32)
            for i, place in enumerate(box_places(box_base, s)):
                weight = beta[pl.ds(pl.multiple_of(s * 40 + i * 8, 8), 8), :]
                total = total + weight * grid[place, :]
            sums[pl.ds(pl.multiple_of(s * 8, 8), 8), :] = total
        return carry

    lax.fori_loop(0, SLOTS // 4, project, 0)
    totals = jnp.sum(sums[...].reshape(SLOTS, 8, 128), axis=1)
    row = lax.broadcasted_iota(jnp.int32, (8, 128), 0)
    column = lax.broadcasted_iota(jnp.int32, (8, 128), 1)
    chooser = jnp.where(row == column // 64, 1.0, 0.0).astype(bf16)
    partial = exact_dot(chooser, split3(totals), ((1,), (1,)))
    by_atom = exact_dot(split3(partial), atom_table(atoms), ((1,), (1,)))
    for part in range(2):
        for r in range(4):
            values = by_atom[part : part + 1, r * 256 : (r + 1) * 256]
            for d in range(N_GA):
                shared[d, part * 4 + r : part * 4 + r + 1, :] = values


def backward_kernel(
    site_row, box_base, shared, strength, atoms, first_matrix, second_matrix, parity, applied_in, beta_in,
    sent, applied, mixed, grid, stage, beta, weights, sems,
):
    beta_copy = pltpu.make_async_copy(beta_in, beta, sems.at[0])
    beta_copy.start()
    total = jnp.sum(shared[...], axis=0)
    by_part = []
    for part in range(2):
        whole_row = jnp.concatenate([total[part * 4 + r : part * 4 + r + 1, :] for r in range(4)], axis=1)
        by_part.append(jnp.broadcast_to(whole_row * strength[...], (64, ATOMS)))
    spread = jnp.concatenate(by_part, axis=0)
    weights[...] = exact_dot(split3(spread), atom_table(atoms), ((1,), (0,))).T
    beta_copy.wait()

    def add_boxes(t, carry):
        for k in range(2):
            s = t * 2 + k
            weight = weights[pl.ds(s, 1), :]
            places = box_places(box_base, s)
            olds = [applied[place, :] for place in places]
            for i in range(5):
                applied[places[i], :] = olds[i] + beta[pl.ds(pl.multiple_of(s * 40 + i * 8, 8), 8), :] * weight
        return carry

    lax.fori_loop(0, SLOTS // 2, add_boxes, 0)

    def along_y(t, carry):
        blocks = []
        for k in range(GROUP):
            start = pl.multiple_of((t * GROUP + k) * ROWS_X, 8)
            top = applied[pl.ds(start, 8), :] + applied[pl.ds(start + N, 8), :]
            blocks.append(jnp.concatenate([top, applied[pl.ds(start + 8, N - 8), :]], axis=0))
        result = fourier_rows(first_matrix[...], blocks)
        for k in range(GROUP):
            mixed[pl.ds((t * GROUP + k) * PITCH, N), :] = result[:, k * 128 : (k + 1) * 128]
        return carry

    lax.fori_loop(0, HALF // GROUP, along_y, 0)

    def along_x(t, carry):
        blocks = []
        for k in range(GROUP):
            pair = t * GROUP + k
            blocks.append(
                exchange_pairs(
                    mixed[pl.ds(2 * pair, HALF, stride=PITCH), :], mixed[pl.ds(2 * pair + 1, HALF, stride=PITCH), :]
                )
            )
        result = fourier_rows(second_matrix[...], blocks)
        for k in range(GROUP):
            grid[pl.ds(pl.multiple_of((t * GROUP + k) * N, 16), N), :] = result[:, k * 128 : (k + 1) * 128]
        return carry

    lax.fori_loop(0, HALF // GROUP, along_x, 0)

    def pick(t, carry):
        base = t * 64
        for k in range(64):
            stage[pl.ds(base + k, 1), :] = grid[pl.ds(site_row[base + k], 1), :]
        return carry

    lax.fori_loop(0, NCOL // 64, pick, 0)
    upper = lax.broadcasted_iota(jnp.int32, (8, 128), 0) < 4

    def transpose(d, carry):
        for j in range(COLS // 128):
            turned = stage[pl.ds(pl.multiple_of(d * COLS + j * 128, 128), 128), :].T
            is_odd = parity[pl.ds(d * (COLS // 128) + j, 1), :] > 0
            real = jnp.where(is_odd, turned[32:56], turned[0:24])
            imag = jnp.where(is_odd, turned[96:120], turned[64:88])
            rest = jnp.where(upper, real[16:24], pltpu.roll(imag[16:24], 4, 0))
            sent[d, :, j * 128 : (j + 1) * 128] = jnp.concatenate([real[0:16], imag[0:16], rest], axis=0)
        return carry

    lax.fori_loop(0, N_GA, transpose, 0)


def whole(space=pltpu.VMEM):
    return pl.BlockSpec(memory_space=space)


def frequency(index):
    return jnp.where(index < HALF, index, index - N).astype(f32)


def on_device(trial_bands, basis_bands, column_sites, potential, box_cells, box_atom, box_beta, strength):
    forward_depth, backward_depth = depth_matrices()
    bands = lax.axis_size("band")
    core = lax.axis_index("band") % 2
    halves = basis_bands.reshape(2, 2, HALF, COLS)
    swap = [(i, i ^ 1) for i in range(bands)]
    kept = jnp.where(core == 0, halves[:, 0], halves[:, 1])
    given = jnp.where(core == 0, halves[:, 1], halves[:, 0])
    taken = lax.ppermute(given, "band", swap)
    block = jnp.where(core == 0, jnp.stack([kept, taken]), jnp.stack([taken, kept])).reshape(2, N, COLS)
    chip_order = list(range(0, bands // 2, 2)) + list(range(bands // 2 - 1, 0, -2))
    rings = [[2 * chip + k for chip in chip_order] for k in range(2)]
    basis_all = lax.all_gather(block, "band", axis=0, axis_index_groups=rings)
    trial = trial_bands.reshape(2 * N, COLS)
    depth = pl.pallas_call(
        depth_kernel,
        out_shape=jax.ShapeDtypeStruct((2 * N, COLS), f32),
        in_specs=[whole()] * 2,
        out_specs=whole(),
        compiler_params=pltpu.CompilerParams(vmem_limit_bytes=LIMIT),
        name="depth",
    )(jnp.asarray(forward_depth), trial)
    recv = lax.all_to_all(depth.reshape(N_GA, 40, COLS), "ga", split_axis=0, concat_axis=0, tiled=True)

    site_x = column_sites // N
    site_y = column_sites - site_x * N
    corner = box_cells[:, 0]
    corner_plane = corner // (N * N)
    in_plane = corner - corner_plane * (N * N)
    corner_x = in_plane // N
    box_base = (corner_x // 2) * ROWS_X + (in_plane - corner_x * N)
    pot, beta = pl.pallas_call(
        prepare_kernel,
        out_shape=(
            jax.ShapeDtypeStruct((HALF * N, 128), f32),
            jax.ShapeDtypeStruct((SLOTS * 40, 128), f32),
        ),
        in_specs=[whole(pltpu.SMEM)] * 2 + [whole()] * 2,
        out_specs=(whole(pl.ANY), whole(pl.ANY)),
        scratch_shapes=[
            pltpu.VMEM((HALF * N, 128), f32),
            pltpu.VMEM((SLOTS * 40, 128), f32),
            pltpu.SemaphoreType.DMA((6,)),
        ],
        compiler_params=pltpu.CompilerParams(vmem_limit_bytes=LIMIT),
        cost_estimate=pl.CostEstimate(flops=0, bytes_accessed=14000000, transcendentals=0),
        name="prepare",
    )(corner_plane, corner_x % 2, potential, box_beta)
    row_count = HALF * ROWS_X
    applied, shared = pl.pallas_call(
        forward_kernel,
        out_shape=(
            pltpu.VMEM((row_count, 128), f32),
            jax.ShapeDtypeStruct((N_GA, 8, ATOMS // 4), f32),
        ),
        in_specs=[whole(pltpu.SMEM)] * 2 + [whole()] * 4 + [whole(pl.ANY)] * 2,
        out_specs=(whole(), whole()),
        scratch_shapes=[
            pltpu.VMEM((N * N, 128), f32),
            pltpu.VMEM((HALF * PITCH, 128), f32),
            pltpu.VMEM((NCOL, 128), f32),
            pltpu.VMEM((SLOTS * 8, 128), f32),
            pltpu.VMEM((HALF * N, 128), f32),
            pltpu.VMEM((SLOTS * 40, 128), f32),
            pltpu.SemaphoreType.DMA((2,)),
        ],
        compiler_params=pltpu.CompilerParams(vmem_limit_bytes=LIMIT - KEPT),
        name="planes_forward",
    )(
        site_y * N + site_x,
        box_base,
        recv,
        jnp.asarray(stage_matrix(1.0, False)),
        jnp.asarray(stage_matrix(1.0, True)),
        box_atom.reshape(1, SLOTS),
        pot,
        beta,
    )
    shared = lax.all_to_all(shared, "ga", split_axis=0, concat_axis=0, tiled=True)
    sent, _ = pl.pallas_call(
        backward_kernel,
        out_shape=(jax.ShapeDtypeStruct((N_GA, 40, COLS), f32), pltpu.VMEM((row_count, 128), f32)),
        in_specs=[whole(pltpu.SMEM)] * 2 + [whole()] * 7 + [whole(pl.ANY)],
        out_specs=(whole(), whole()),
        input_output_aliases={8: 1},
        scratch_shapes=[
            pltpu.VMEM((HALF * PITCH, 128), f32),
            pltpu.VMEM((HALF * N, 128), f32),
            pltpu.VMEM((NCOL, 128), f32),
            pltpu.VMEM((SLOTS * 40, 128), f32),
            pltpu.VMEM((SLOTS, 128), f32),
            pltpu.SemaphoreType.DMA((1,)),
        ],
        compiler_params=pltpu.CompilerParams(vmem_limit_bytes=LIMIT - KEPT),
        name="planes_backward",
    )(
        (site_y // 2) * N + site_x,
        box_base,
        shared,
        strength.reshape(1, ATOMS),
        box_atom.reshape(1, SLOTS),
        jnp.asarray(stage_matrix(-1.0, False)),
        jnp.asarray(stage_matrix(-1.0, True)),
        (site_y % 2).reshape(NCOL // 128, 128),
        applied,
        beta,
    )
    returned = lax.all_to_all(sent, "ga", split_axis=0, concat_axis=0, tiled=True)
    own = lax.dynamic_slice_in_dim(column_sites, lax.axis_index("ga") * COLS, COLS)
    plane_kinetic = (2.0 / float(N * N)) * (frequency(own // N) ** 2 + frequency(own % N) ** 2)
    core_number = core.reshape(1)
    result, away = pl.pallas_call(
        finish_kernel,
        out_shape=(jax.ShapeDtypeStruct((2 * N, COLS), f32), jax.ShapeDtypeStruct((N, COLS), f32)),
        in_specs=[whole(pltpu.SMEM)] + [whole()] * 4,
        out_specs=(whole(), whole()),
        compiler_params=pltpu.CompilerParams(vmem_limit_bytes=LIMIT),
        name="finish",
    )(
        core_number,
        jnp.asarray(backward_depth),
        returned.reshape(2 * N, COLS),
        trial,
        plane_kinetic.reshape(1, COLS),
    )
    brought = lax.ppermute(away, "band", swap)
    gram = pl.pallas_call(
        gram_kernel,
        out_shape=jax.ShapeDtypeStruct((16, 2 * bands), f32),
        in_specs=[whole(pltpu.SMEM)] + [whole()] * 2 + [whole(pl.ANY)],
        out_specs=whole(),
        scratch_shapes=[
            pltpu.VMEM((bands // 2, 2, N, COLS), f32),
            pltpu.VMEM((2 * bands, 128), f32),
            pltpu.VMEM((2 * bands, 128), f32),
            pltpu.SemaphoreType.DMA((bands // 2,)),
        ],
        compiler_params=pltpu.CompilerParams(vmem_limit_bytes=LIMIT),
        name="gram",
    )(core_number, result, brought, basis_all)
    chip_group = [[(2 * chip + k) * N_GA + g for k in range(2) for g in range(N_GA)] for chip in range(bands // 2)]
    gram = lax.all_to_all(
        gram, ("band", "ga"), split_axis=0, concat_axis=0, tiled=True, axis_index_groups=chip_group
    )
    gram = (jnp.sum(gram, axis=0) * (1.0 / math.sqrt(N * NCOL))).reshape(bands, 2).T
    return (result.reshape(trial_bands.shape), gram[:, :, None])


def solution(mesh):
    placed = (
        P("band", None, None, "ga"),
        P("band", None, None, "ga"),
        P(),
        P("ga", None, None),
        P("ga", None),
        P("ga"),
        P("ga", None),
        P(),
    )
    return jax.shard_map(
        on_device,
        mesh=mesh,
        in_specs=placed,
        out_specs=(P("band", None, None, "ga"), P(None, None, "band")),
        check_vma=False,
    )
```

```python
import math

import jax
import jax.numpy as jnp
import numpy as np
from jax import lax
from jax.experimental import pallas as pl
from jax.experimental.pallas import tpu as pltpu
from jax.sharding import PartitionSpec as P

N = 160
HALF = N // 2
N_GA = 8
PLANES = N // N_GA
NCOL = 5120
COLS = NCOL // N_GA
SLOTS = 192
ROWS_X = N + 8
ATOMS = 1024
GROUP = 40
PITCH = 164
MIB = 1024 * 1024
bf16 = jnp.bfloat16
f32 = jnp.float32


def split_np(matrix):
    high = np.asarray(matrix, np.float32).astype(jnp.bfloat16)
    low = (np.asarray(matrix, np.float64) - high.astype(np.float64)).astype(np.float32).astype(jnp.bfloat16)
    return high, low


def fourier(orient):
    index = np.arange(N)
    angle = (np.outer(index, index) % N) * (2.0 * np.pi / N)
    return np.cos(angle), orient * np.sin(angle)


def stage_matrix(orient, paired):
    cosine, sine = fourier(orient)
    if paired:
        order = np.concatenate([np.arange(0, N, 2), np.arange(1, N, 2)])
        cosine, sine = cosine[:, order], sine[:, order]
    ch, cl = split_np(cosine)
    sh, sl = split_np(sine)
    return np.concatenate([ch, sh, ch, sh, cl, sl], axis=1)


def sent_order():
    rows = []
    for d in range(N_GA):
        for part, span in ((0, range(16)), (1, range(16)), (0, range(16, 20)), (1, range(16, 20))):
            rows += [(part, d * PLANES + p) for p in span]
    return rows


def depth_matrices():
    cosine, sine = fourier(1.0)
    full = np.block([[cosine, -sine], [sine, cosine]])
    back = np.block([[cosine, sine], [-sine, cosine]]) / float(N**3)
    order = np.array([part * N + z for part, z in sent_order()])
    tables = []
    for matrix in (full[order], back[:, order]):
        high, low = split_np(matrix)
        tables.append(np.concatenate([high, high, low], axis=1))
    return tables


def lanes():
    return lax.broadcasted_iota(jnp.int32, (1, 128), 1)


def fourier_rows(matrix, blocks):
    lane = lanes()
    sign = jnp.where(lane < 64, -1.0, 1.0).astype(f32)
    pieces = []
    for block in blocks:
        turned = pltpu.roll(block, 64, 1) * sign
        high = block.astype(bf16)
        low = (block - high.astype(f32)).astype(bf16)
        turned_high = turned.astype(bf16)
        turned_low = (turned - turned_high.astype(f32)).astype(bf16)
        pieces.append(jnp.concatenate([high, turned_high, low, turned_low, high, turned_high], axis=0))
    right = pieces[0] if len(pieces) == 1 else jnp.concatenate(pieces, axis=1)
    return jnp.dot(matrix, right, preferred_element_type=f32)


def exchange_pairs(first, second):
    odd = (lanes() // 32) % 2 == 1
    even_rows = jnp.where(odd, pltpu.roll(second, 32, 1), first)
    odd_rows = jnp.where(odd, second, pltpu.roll(first, 96, 1))
    return jnp.concatenate([even_rows, odd_rows], axis=0)


def split3(values):
    high = values.astype(bf16)
    rest = values - high.astype(f32)
    middle = rest.astype(bf16)
    return high, middle, (rest - middle.astype(f32)).astype(bf16)


def exact_dot(first, second, contract):
    total = None
    if isinstance(first, tuple):
        terms = [(piece, second) for piece in first]
    else:
        terms = [(first, piece) for piece in second]
    for left, right in terms:
        product = lax.dot_general(left, right, (contract, ((), ())), preferred_element_type=f32)
        total = product if total is None else total + product
    return total


def atom_table(atoms):
    row = lax.broadcasted_iota(jnp.int32, (ATOMS, SLOTS), 0)
    return jnp.where(atoms[...] == row, 1.0, 0.0).astype(bf16)


def box_places(box_base, s):
    places = []
    for i in range(5):
        start = box_base[s] + i * ROWS_X
        places.append(pl.ds(jnp.where(start >= HALF * ROWS_X, start - HALF * ROWS_X, start), 8))
    return places


def depth_product(matrix, values):
    high = values.astype(bf16)
    low = (values - high.astype(f32)).astype(bf16)
    return jnp.dot(matrix, jnp.concatenate([high, low, high], axis=0), preferred_element_type=f32)


def depth_kernel(matrix, values, out):
    out[...] = depth_product(matrix[...], values[...])


def prepare_kernel(
    box_plane, box_odd, potential, box_beta, potential_out, beta_out, rows, table, sems
):
    copies = []

    def send(source, target, start, size):
        span = pl.ds(start, size)
        copies.append(pltpu.make_async_copy(source.at[span], target.at[span], sems.at[len(copies)]))
        copies[-1].start()

    lane = lanes()
    lane_odd = (lane // 32) % 2 == 1
    lane_plane = lane % 32
    local_box = lax.broadcasted_iota(jnp.int32, (16, 128), 0) % 8
    local_plane = lane_plane - lax.broadcasted_iota(jnp.int32, (16, 128), 0) // 8
    nothing = jnp.zeros((8, 128), f32)

    def spread(t, carry):
        values = box_beta[pl.ds(pl.multiple_of(t * 8, 8), 8), :]
        both = jnp.concatenate([values, pltpu.roll(values, 64, 1)], axis=0)
        high = both.astype(bf16).astype(f32)
        left = jnp.concatenate([high, both - high], axis=0).T[0:64].astype(bf16)
        masks = []
        for k in range(8):
            hit = (local_box == k) & (local_plane == box_plane[t * 8 + k])
            masks.append(jnp.where(hit, 1.0, 0.0))
        mask = jnp.concatenate(masks, axis=1)
        right = jnp.concatenate([mask, mask], axis=0).astype(bf16)
        lines = jnp.dot(left, right, preferred_element_type=f32)
        for k in range(8):
            s = t * 8 + k
            shifted = box_odd[s] > 0
            line = [lines[x * 8 : x * 8 + 8, k * 128 : (k + 1) * 128] for x in range(8)]
            for i in range(5):
                even = line[2 * i] if i < 4 else nothing
                straight = jnp.where(lane_odd, line[2 * i + 1], even) if i < 4 else nothing
                moved = jnp.where(lane_odd, even, line[2 * i - 1] if i > 0 else nothing)
                table[pl.ds(pl.multiple_of(s * 40 + i * 8, 8), 8), :] = jnp.where(shifted, moved, straight)
        return carry

    def spread_two(t, carry):
        spread(2 * t, 0)
        spread(2 * t + 1, 0)
        return carry

    for piece in range(2):
        lax.fori_loop(piece * 6, piece * 6 + 6, spread_two, 0)
        send(table, beta_out, piece * SLOTS * 20, SLOTS * 20)
    zero = jnp.zeros((8, N), f32)
    for piece in range(4):
        for k in range(HALF // 4):
            pair = piece * (HALF // 4) + k
            pieces = []
            for half in range(2):
                plane = potential[:, 2 * pair + half, :]
                pieces += [plane[0:8], plane[8:16], jnp.concatenate([plane[16:20], zero[0:4]], axis=0), zero]
            stacked = jnp.concatenate(pieces + pieces, axis=0)
            rows[pair * N : pair * N + 128, :] = stacked[:, 0:128].T
            rows[pair * N + 128 : pair * N + N, :] = stacked[:, 128:N].T
        send(rows, potential_out, piece * (HALF // 4) * N, (HALF // 4) * N)
    for copy in copies:
        copy.wait()


def finish_kernel(core, matrix, returned, trial, plane_kinetic, result, away):
    depth = lax.broadcasted_iota(jnp.int32, (N, 1), 0)
    depth = jnp.where(depth < HALF, depth, depth - N).astype(f32)
    kinetic = (2.0 / float(N * N)) * (depth * depth) + plane_kinetic[...]
    spectrum = depth_product(matrix[...], returned[...])
    first = core[0] == 0
    for part in range(2):
        rows = slice(part * N, part * N + N)
        values = spectrum[rows] + kinetic * trial[rows, :]
        result[rows, :] = values
        away[part * HALF : part * HALF + HALF, :] = jnp.where(first, values[HALF:N], values[0:HALF])


def gram_kernel(core, result, brought, basis_all, gram, basis, own_sums, other_sums, sems):
    chips = basis_all.shape[0]

    def fetch(m):
        return pltpu.make_async_copy(basis_all.at[m], basis.at[m], sems.at[m])

    for m in range(chips):
        fetch(m).start()
    half = core[0] * HALF

    def one_chip(m, carry):
        fetch(m).wait()
        chip = jnp.where(m < chips // 2, 2 * m, 2 * chips - 1 - 2 * m)

        def rows(t, totals):
            totals = list(totals)
            row = pl.multiple_of(t * 8, 8)
            here = (pl.ds(row, 8), pl.ds(row + HALF, 8))
            mine = (pl.ds(pl.multiple_of(half + row, 8), 8), pl.ds(pl.multiple_of(half + N + row, 8), 8))
            for j in range(COLS // 128):
                tile = slice(j * 128, (j + 1) * 128)
                rights = [(result[mine[0], tile], result[mine[1], tile]), (brought[here[0], tile], brought[here[1], tile])]
                for slot in range(2):
                    left_real, left_imag = basis[m, slot, here[0], tile], basis[m, slot, here[1], tile]
                    for n, (real, imag) in enumerate(rights):
                        at = n * 4 + slot * 2
                        totals[at] = totals[at] + (left_real * real + left_imag * imag)
                        totals[at + 1] = totals[at + 1] + (left_real * imag - left_imag * real)
            return tuple(totals)

        totals = lax.fori_loop(0, HALF // 8, rows, (jnp.zeros((8, 128), f32),) * 8)
        for at in range(4):
            own_sums[pl.ds(chip * 4 + at, 1), :] = jnp.sum(totals[at], axis=0, keepdims=True)
            other_sums[pl.ds(chip * 4 + at, 1), :] = jnp.sum(totals[4 + at], axis=0, keepdims=True)
        return carry

    lax.fori_loop(0, chips, one_chip, 0)
    ones = jnp.ones((8, 128), bf16)
    own = exact_dot(ones, split3(own_sums[...]), ((1,), (1,)))
    other = exact_dot(ones, split3(other_sums[...]), ((1,), (1,)))
    first = core[0] == 0
    gram[0:8, :] = jnp.where(first, own, other)
    gram[8:16, :] = jnp.where(first, other, own)


def forward_kernel(
    site_row, box_base, recv, first_matrix, second_matrix, atoms, potential_in, beta_in,
    applied, shared, grid, mixed, stage, sums, potential, beta, sems,
):
    potential_copy = pltpu.make_async_copy(potential_in, potential, sems.at[0])
    beta_copy = pltpu.make_async_copy(beta_in, beta, sems.at[1])
    potential_copy.start()
    beta_copy.start()

    def transpose(d, carry):
        for j in range(COLS // 128):
            block = recv[d, :, j * 128 : (j + 1) * 128]
            real, imag, rest = block[0:16], block[16:32], block[32:40]
            swapped = pltpu.roll(rest, 4, 0)
            zero = jnp.zeros((8, 128), f32)
            stacked = jnp.concatenate(
                [real, rest, zero, real, rest, zero, imag, swapped, zero, imag, swapped, zero], axis=0
            )
            stage[pl.ds(pl.multiple_of(d * COLS + j * 128, 128), 128), :] = stacked.T
        return carry

    lax.fori_loop(0, N_GA, transpose, 0)

    def clear(t, carry):
        grid[pl.ds(pl.multiple_of(t * 256, 256), 256), :] = jnp.zeros((256, 128), f32)
        return carry

    lax.fori_loop(0, N * N // 256, clear, 0)

    def place(t, carry):
        base = t * 64
        for k in range(64):
            grid[pl.ds(site_row[base + k], 1), :] = stage[pl.ds(base + k, 1), :]
        return carry

    lax.fori_loop(0, NCOL // 64, place, 0)

    odd = (lanes() // 32) % 2 == 1

    def along_x(t, carry):
        blocks = []
        for k in range(GROUP):
            start = pl.multiple_of((t * GROUP + k) * 2 * N, 16)
            even_y = grid[pl.ds(start, N), :]
            odd_y = grid[pl.ds(start + N, N), :]
            blocks.append(jnp.where(odd, odd_y, even_y))
        result = fourier_rows(first_matrix[...], blocks)
        for k in range(GROUP):
            mixed[pl.ds((t * GROUP + k) * PITCH, N), :] = result[:, k * 128 : (k + 1) * 128]
        return carry

    lax.fori_loop(0, HALF // GROUP, along_x, 0)
    potential_copy.wait()

    def along_y(t, carry):
        blocks = []
        for k in range(GROUP):
            pair = t * GROUP + k
            blocks.append(
                exchange_pairs(
                    mixed[pl.ds(2 * pair, HALF, stride=PITCH), :], mixed[pl.ds(2 * pair + 1, HALF, stride=PITCH), :]
                )
            )
        result = fourier_rows(second_matrix[...], blocks)
        for k in range(GROUP):
            pair = t * GROUP + k
            values = result[:, k * 128 : (k + 1) * 128]
            start = pl.multiple_of(pair * ROWS_X, 8)
            grid[pl.ds(start, N), :] = values
            grid[pl.ds(start + N, 8), :] = values[0:8]
            applied[pl.ds(start, N), :] = values * potential[pl.ds(pl.multiple_of(pair * N, 16), N), :]
            applied[pl.ds(start + N, 8), :] = jnp.zeros((8, 128), f32)
        return carry

    for t in range(HALF // GROUP):
        along_y(t, 0)
    beta_copy.wait()

    def project(t, carry):
        for k in range(4):
            s = t * 4 + k
            total = jnp.zeros((8, 128), f32)
            for i, place in enumerate(box_places(box_base, s)):
                weight = beta[pl.ds(pl.multiple_of(s * 40 + i * 8, 8), 8), :]
                total = total + weight * grid[place, :]
            sums[pl.ds(pl.multiple_of(s * 8, 8), 8), :] = total
        return carry

    lax.fori_loop(0, SLOTS // 4, project, 0)
    totals = jnp.sum(sums[...].reshape(SLOTS, 8, 128), axis=1)
    row = lax.broadcasted_iota(jnp.int32, (8, 128), 0)
    column = lax.broadcasted_iota(jnp.int32, (8, 128), 1)
    chooser = jnp.where(row == column // 64, 1.0, 0.0).astype(bf16)
    partial = exact_dot(chooser, split3(totals), ((1,), (1,)))
    by_atom = exact_dot(split3(partial), atom_table(atoms), ((1,), (1,)))
    for part in range(2):
        for r in range(4):
            values = by_atom[part : part + 1, r * 256 : (r + 1) * 256]
            for d in range(N_GA):
                shared[d, part * 4 + r : part * 4 + r + 1, :] = values


def backward_kernel(
    site_row, box_base, shared, strength, atoms, first_matrix, second_matrix, parity, applied_in, beta_in,
    sent, applied, mixed, grid, stage, beta, weights, sems,
):
    beta_copy = pltpu.make_async_copy(beta_in, beta, sems.at[0])
    beta_copy.start()
    total = jnp.sum(shared[...], axis=0)
    by_part = []
    for part in range(2):
        whole_row = jnp.concatenate([total[part * 4 + r : part * 4 + r + 1, :] for r in range(4)], axis=1)
        by_part.append(jnp.broadcast_to(whole_row * strength[...], (64, ATOMS)))
    spread = jnp.concatenate(by_part, axis=0)
    weights[...] = exact_dot(split3(spread), atom_table(atoms), ((1,), (0,))).T
    beta_copy.wait()

    def add_boxes(t, carry):
        for k in range(2):
            s = t * 2 + k
            weight = weights[pl.ds(s, 1), :]
            places = box_places(box_base, s)
            olds = [applied[place, :] for place in places]
            for i in range(5):
                applied[places[i], :] = olds[i] + beta[pl.ds(pl.multiple_of(s * 40 + i * 8, 8), 8), :] * weight
        return carry

    lax.fori_loop(0, SLOTS // 2, add_boxes, 0)

    def along_y(t, carry):
        blocks = []
        for k in range(GROUP):
            start = pl.multiple_of((t * GROUP + k) * ROWS_X, 8)
            top = applied[pl.ds(start, 8), :] + applied[pl.ds(start + N, 8), :]
            blocks.append(jnp.concatenate([top, applied[pl.ds(start + 8, N - 8), :]], axis=0))
        result = fourier_rows(first_matrix[...], blocks)
        for k in range(GROUP):
            mixed[pl.ds((t * GROUP + k) * PITCH, N), :] = result[:, k * 128 : (k + 1) * 128]
        return carry

    lax.fori_loop(0, HALF // GROUP, along_y, 0)

    def along_x(t, carry):
        blocks = []
        for k in range(GROUP):
            pair = t * GROUP + k
            blocks.append(
                exchange_pairs(
                    mixed[pl.ds(2 * pair, HALF, stride=PITCH), :], mixed[pl.ds(2 * pair + 1, HALF, stride=PITCH), :]
                )
            )
        result = fourier_rows(second_matrix[...], blocks)
        for k in range(GROUP):
            grid[pl.ds(pl.multiple_of((t * GROUP + k) * N, 16), N), :] = result[:, k * 128 : (k + 1) * 128]
        return carry

    lax.fori_loop(0, HALF // GROUP, along_x, 0)

    def pick(t, carry):
        base = t * 64
        for k in range(64):
            stage[pl.ds(base + k, 1), :] = grid[pl.ds(site_row[base + k], 1), :]
        return carry

    lax.fori_loop(0, NCOL // 64, pick, 0)
    upper = lax.broadcasted_iota(jnp.int32, (8, 128), 0) < 4

    def transpose(d, carry):
        for j in range(COLS // 128):
            turned = stage[pl.ds(pl.multiple_of(d * COLS + j * 128, 128), 128), :].T
            is_odd = parity[pl.ds(d * (COLS // 128) + j, 1), :] > 0
            real = jnp.where(is_odd, turned[32:56], turned[0:24])
            imag = jnp.where(is_odd, turned[96:120], turned[64:88])
            rest = jnp.where(upper, real[16:24], pltpu.roll(imag[16:24], 4, 0))
            sent[d, :, j * 128 : (j + 1) * 128] = jnp.concatenate([real[0:16], imag[0:16], rest], axis=0)
        return carry

    lax.fori_loop(0, N_GA, transpose, 0)


def whole(space=pltpu.VMEM):
    return pl.BlockSpec(memory_space=space)


def frequency(index):
    return jnp.where(index < HALF, index, index - N).astype(f32)


def on_device(trial_bands, basis_bands, column_sites, potential, box_cells, box_atom, box_beta, strength):
    forward_depth, backward_depth = depth_matrices()
    bands = lax.axis_size("band")
    core = lax.axis_index("band") % 2
    halves = basis_bands.reshape(2, 2, HALF, COLS)
    swap = [(i, i ^ 1) for i in range(bands)]
    kept = jnp.where(core == 0, halves[:, 0], halves[:, 1])
    given = jnp.where(core == 0, halves[:, 1], halves[:, 0])
    trial = trial_bands.reshape(2 * N, COLS)
    taken = lax.ppermute(given, "band", swap)
    depth = pl.pallas_call(
        depth_kernel,
        out_shape=jax.ShapeDtypeStruct((2 * N, COLS), f32),
        in_specs=[whole()] * 2,
        out_specs=whole(),
        compiler_params=pltpu.CompilerParams(vmem_limit_bytes=60 * MIB),
        cost_estimate=pl.CostEstimate(flops=2000000000, bytes_accessed=8000000, transcendentals=0),
        name="depth",
    )(jnp.asarray(forward_depth), trial)
    taken, depth = lax.optimization_barrier((taken, depth))
    block = jnp.where(core == 0, jnp.stack([kept, taken]), jnp.stack([taken, kept])).reshape(2, N, COLS)
    depth, block = lax.optimization_barrier((depth, block))
    chip_order = list(range(0, bands // 2, 2)) + list(range(bands // 2 - 1, 0, -2))
    rings = [[2 * chip + k for chip in chip_order] for k in range(2)]
    basis_all = lax.all_gather(block, "band", axis=0, axis_index_groups=rings)
    recv = lax.all_to_all(depth.reshape(N_GA, 40, COLS), "ga", split_axis=0, concat_axis=0, tiled=True)

    site_x = column_sites // N
    site_y = column_sites - site_x * N
    corner = box_cells[:, 0]
    corner_plane = corner // (N * N)
    in_plane = corner - corner_plane * (N * N)
    corner_x = in_plane // N
    box_base = (corner_x // 2) * ROWS_X + (in_plane - corner_x * N)
    pot, beta = pl.pallas_call(
        prepare_kernel,
        out_shape=(
            jax.ShapeDtypeStruct((HALF * N, 128), f32),
            jax.ShapeDtypeStruct((SLOTS * 40, 128), f32),
        ),
        in_specs=[whole(pltpu.SMEM)] * 2 + [whole()] * 2,
        out_specs=(whole(pl.ANY), whole(pl.ANY)),
        scratch_shapes=[
            pltpu.VMEM((HALF * N, 128), f32),
            pltpu.VMEM((SLOTS * 40, 128), f32),
            pltpu.SemaphoreType.DMA((6,)),
        ],
        compiler_params=pltpu.CompilerParams(vmem_limit_bytes=57 * MIB),
        cost_estimate=pl.CostEstimate(flops=0, bytes_accessed=14000000, transcendentals=0),
        name="prepare",
    )(corner_plane, corner_x % 2, potential, box_beta)
    row_count = HALF * ROWS_X
    applied, shared = pl.pallas_call(
        forward_kernel,
        out_shape=(
            pltpu.VMEM((row_count, 128), f32),
            jax.ShapeDtypeStruct((N_GA, 8, ATOMS // 4), f32),
        ),
        in_specs=[whole(pltpu.SMEM)] * 2 + [whole()] * 4 + [whole(pl.ANY)] * 2,
        out_specs=(whole(), whole()),
        scratch_shapes=[
            pltpu.VMEM((N * N, 128), f32),
            pltpu.VMEM((HALF * PITCH, 128), f32),
            pltpu.VMEM((NCOL, 128), f32),
            pltpu.VMEM((SLOTS * 8, 128), f32),
            pltpu.VMEM((HALF * N, 128), f32),
            pltpu.VMEM((SLOTS * 40, 128), f32),
            pltpu.SemaphoreType.DMA((2,)),
        ],
        compiler_params=pltpu.CompilerParams(vmem_limit_bytes=50 * MIB),
        name="planes_forward",
    )(
        site_y * N + site_x,
        box_base,
        recv,
        jnp.asarray(stage_matrix(1.0, False)),
        jnp.asarray(stage_matrix(1.0, True)),
        box_atom.reshape(1, SLOTS),
        pot,
        beta,
    )
    shared = lax.all_to_all(shared, "ga", split_axis=0, concat_axis=0, tiled=True)
    sent, _ = pl.pallas_call(
        backward_kernel,
        out_shape=(jax.ShapeDtypeStruct((N_GA, 40, COLS), f32), pltpu.VMEM((row_count, 128), f32)),
        in_specs=[whole(pltpu.SMEM)] * 2 + [whole()] * 7 + [whole(pl.ANY)],
        out_specs=(whole(), whole()),
        input_output_aliases={8: 1},
        scratch_shapes=[
            pltpu.VMEM((HALF * PITCH, 128), f32),
            pltpu.VMEM((HALF * N, 128), f32),
            pltpu.VMEM((NCOL, 128), f32),
            pltpu.VMEM((SLOTS * 40, 128), f32),
            pltpu.VMEM((SLOTS, 128), f32),
            pltpu.SemaphoreType.DMA((1,)),
        ],
        compiler_params=pltpu.CompilerParams(vmem_limit_bytes=44 * MIB),
        name="planes_backward",
    )(
        (site_y // 2) * N + site_x,
        box_base,
        shared,
        strength.reshape(1, ATOMS),
        box_atom.reshape(1, SLOTS),
        jnp.asarray(stage_matrix(-1.0, False)),
        jnp.asarray(stage_matrix(-1.0, True)),
        (site_y % 2).reshape(NCOL // 128, 128),
        applied,
        beta,
    )
    returned = lax.all_to_all(sent, "ga", split_axis=0, concat_axis=0, tiled=True)
    own = lax.dynamic_slice_in_dim(column_sites, lax.axis_index("ga") * COLS, COLS)
    plane_kinetic = (2.0 / float(N * N)) * (frequency(own // N) ** 2 + frequency(own % N) ** 2)
    core_number = core.reshape(1)
    result, away = pl.pallas_call(
        finish_kernel,
        out_shape=(jax.ShapeDtypeStruct((2 * N, COLS), f32), jax.ShapeDtypeStruct((N, COLS), f32)),
        in_specs=[whole(pltpu.SMEM)] + [whole()] * 4,
        out_specs=(whole(), whole()),
        compiler_params=pltpu.CompilerParams(vmem_limit_bytes=57 * MIB),
        name="finish",
    )(
        core_number,
        jnp.asarray(backward_depth),
        returned.reshape(2 * N, COLS),
        trial,
        plane_kinetic.reshape(1, COLS),
    )
    brought = lax.ppermute(away, "band", swap)
    gram = pl.pallas_call(
        gram_kernel,
        out_shape=jax.ShapeDtypeStruct((16, 2 * bands), f32),
        in_specs=[whole(pltpu.SMEM)] + [whole()] * 2 + [whole(pl.ANY)],
        out_specs=whole(),
        scratch_shapes=[
            pltpu.VMEM((bands // 2, 2, N, COLS), f32),
            pltpu.VMEM((2 * bands, 128), f32),
            pltpu.VMEM((2 * bands, 128), f32),
            pltpu.SemaphoreType.DMA((bands // 2,)),
        ],
        compiler_params=pltpu.CompilerParams(vmem_limit_bytes=60 * MIB),
        name="gram",
    )(core_number, result, brought, basis_all)
    chip_group = [[(2 * chip + k) * N_GA + g for k in range(2) for g in range(N_GA)] for chip in range(bands // 2)]
    gram = lax.all_to_all(
        gram, ("band", "ga"), split_axis=0, concat_axis=0, tiled=True, axis_index_groups=chip_group
    )
    gram = (jnp.sum(gram, axis=0) * (1.0 / math.sqrt(N * NCOL))).reshape(bands, 2).T
    return (result.reshape(trial_bands.shape), gram[:, :, None])


def solution(mesh):
    placed = (
        P("band", None, None, "ga"),
        P("band", None, None, "ga"),
        P(),
        P("ga", None, None),
        P("ga", None),
        P("ga"),
        P("ga", None),
        P(),
    )
    return jax.shard_map(
        on_device,
        mesh=mesh,
        in_specs=placed,
        out_specs=(P("band", None, None, "ga"), P(None, None, "band")),
        check_vma=False,
    )
```

```python
import math

import jax
import jax.numpy as jnp
import numpy as np
from jax import lax
from jax.experimental import pallas as pl
from jax.experimental.pallas import tpu as pltpu
from jax.sharding import PartitionSpec as P

N = 160
HALF = N // 2
N_GA = 8
PLANES = N // N_GA
NCOL = 5120
COLS = NCOL // N_GA
SLOTS = 192
ROWS_X = N + 8
ATOMS = 1024
GROUP = 40
PITCH = 164
MIB = 1024 * 1024
bf16 = jnp.bfloat16
f32 = jnp.float32


def split_np(matrix):
    high = np.asarray(matrix, np.float32).astype(jnp.bfloat16)
    low = (np.asarray(matrix, np.float64) - high.astype(np.float64)).astype(np.float32).astype(jnp.bfloat16)
    return high, low


def fourier(orient):
    index = np.arange(N)
    angle = (np.outer(index, index) % N) * (2.0 * np.pi / N)
    return np.cos(angle), orient * np.sin(angle)


def stage_matrix(orient, paired):
    cosine, sine = fourier(orient)
    if paired:
        order = np.concatenate([np.arange(0, N, 2), np.arange(1, N, 2)])
        cosine, sine = cosine[:, order], sine[:, order]
    ch, cl = split_np(cosine)
    sh, sl = split_np(sine)
    return np.concatenate([ch, sh, ch, sh, cl, sl], axis=1)


def sent_order():
    rows = []
    for d in range(N_GA):
        for part, span in ((0, range(16)), (1, range(16)), (0, range(16, 20)), (1, range(16, 20))):
            rows += [(part, d * PLANES + p) for p in span]
    return rows


def depth_matrices():
    cosine, sine = fourier(1.0)
    full = np.block([[cosine, -sine], [sine, cosine]])
    back = np.block([[cosine, sine], [-sine, cosine]]) / float(N**3)
    order = np.array([part * N + z for part, z in sent_order()])
    tables = []
    for matrix in (full[order], back[:, order]):
        high, low = split_np(matrix)
        tables.append(np.concatenate([high, high, low], axis=1))
    return tables


def lanes():
    return lax.broadcasted_iota(jnp.int32, (1, 128), 1)


def fourier_rows(matrix, blocks):
    lane = lanes()
    sign = jnp.where(lane < 64, -1.0, 1.0).astype(f32)
    pieces = []
    for block in blocks:
        turned = pltpu.roll(block, 64, 1) * sign
        high = block.astype(bf16)
        low = (block - high.astype(f32)).astype(bf16)
        turned_high = turned.astype(bf16)
        turned_low = (turned - turned_high.astype(f32)).astype(bf16)
        pieces.append(jnp.concatenate([high, turned_high, low, turned_low, high, turned_high], axis=0))
    right = pieces[0] if len(pieces) == 1 else jnp.concatenate(pieces, axis=1)
    return jnp.dot(matrix, right, preferred_element_type=f32)


def exchange_pairs(first, second):
    odd = (lanes() // 32) % 2 == 1
    even_rows = jnp.where(odd, pltpu.roll(second, 32, 1), first)
    odd_rows = jnp.where(odd, second, pltpu.roll(first, 96, 1))
    return jnp.concatenate([even_rows, odd_rows], axis=0)


def split3(values):
    high = values.astype(bf16)
    rest = values - high.astype(f32)
    middle = rest.astype(bf16)
    return high, middle, (rest - middle.astype(f32)).astype(bf16)


def exact_dot(first, second, contract):
    total = None
    if isinstance(first, tuple):
        terms = [(piece, second) for piece in first]
    else:
        terms = [(first, piece) for piece in second]
    for left, right in terms:
        product = lax.dot_general(left, right, (contract, ((), ())), preferred_element_type=f32)
        total = product if total is None else total + product
    return total


def atom_table(atoms):
    row = lax.broadcasted_iota(jnp.int32, (ATOMS, SLOTS), 0)
    return jnp.where(atoms[...] == row, 1.0, 0.0).astype(bf16)


def box_places(box_base, s):
    places = []
    for i in range(5):
        start = box_base[s] + i * ROWS_X
        places.append(pl.ds(jnp.where(start >= HALF * ROWS_X, start - HALF * ROWS_X, start), 8))
    return places


def depth_product(matrix, values):
    high = values.astype(bf16)
    low = (values - high.astype(f32)).astype(bf16)
    return jnp.dot(matrix, jnp.concatenate([high, low, high], axis=0), preferred_element_type=f32)


def depth_kernel(matrix, values, out):
    out[...] = depth_product(matrix[...], values[...])


def prepare_kernel(
    box_plane, box_odd, potential, box_beta, potential_out, beta_out, rows, table, sems
):
    copies = []

    def send(source, target, start, size):
        span = pl.ds(start, size)
        copies.append(pltpu.make_async_copy(source.at[span], target.at[span], sems.at[len(copies)]))
        copies[-1].start()

    lane = lanes()
    lane_odd = (lane // 32) % 2 == 1
    lane_plane = lane % 32
    local_box = lax.broadcasted_iota(jnp.int32, (16, 128), 0) % 8
    local_plane = lane_plane - lax.broadcasted_iota(jnp.int32, (16, 128), 0) // 8
    nothing = jnp.zeros((8, 128), f32)

    def spread(t, carry):
        values = box_beta[pl.ds(pl.multiple_of(t * 8, 8), 8), :]
        both = jnp.concatenate([values, pltpu.roll(values, 64, 1)], axis=0)
        high = both.astype(bf16).astype(f32)
        left = jnp.concatenate([high, both - high], axis=0).T[0:64].astype(bf16)
        masks = []
        for k in range(8):
            hit = (local_box == k) & (local_plane == box_plane[t * 8 + k])
            masks.append(jnp.where(hit, 1.0, 0.0))
        mask = jnp.concatenate(masks, axis=1)
        right = jnp.concatenate([mask, mask], axis=0).astype(bf16)
        lines = jnp.dot(left, right, preferred_element_type=f32)
        for k in range(8):
            s = t * 8 + k
            shifted = box_odd[s] > 0
            line = [lines[x * 8 : x * 8 + 8, k * 128 : (k + 1) * 128] for x in range(8)]
            for i in range(5):
                even = line[2 * i] if i < 4 else nothing
                straight = jnp.where(lane_odd, line[2 * i + 1], even) if i < 4 else nothing
                moved = jnp.where(lane_odd, even, line[2 * i - 1] if i > 0 else nothing)
                table[pl.ds(pl.multiple_of(s * 40 + i * 8, 8), 8), :] = jnp.where(shifted, moved, straight)
        return carry

    def spread_two(t, carry):
        spread(2 * t, 0)
        spread(2 * t + 1, 0)
        return carry

    for piece in range(2):
        lax.fori_loop(piece * 6, piece * 6 + 6, spread_two, 0)
        send(table, beta_out, piece * SLOTS * 20, SLOTS * 20)
    zero = jnp.zeros((8, N), f32)
    for piece in range(4):
        for k in range(HALF // 4):
            pair = piece * (HALF // 4) + k
            pieces = []
            for half in range(2):
                plane = potential[:, 2 * pair + half, :]
                pieces += [plane[0:8], plane[8:16], jnp.concatenate([plane[16:20], zero[0:4]], axis=0), zero]
            stacked = jnp.concatenate(pieces + pieces, axis=0)
            rows[pair * N : pair * N + 128, :] = stacked[:, 0:128].T
            rows[pair * N + 128 : pair * N + N, :] = stacked[:, 128:N].T
        send(rows, potential_out, piece * (HALF // 4) * N, (HALF // 4) * N)
    for copy in copies:
        copy.wait()


def finish_kernel(core, matrix, returned, trial, plane_kinetic, result, away):
    depth = lax.broadcasted_iota(jnp.int32, (N, 1), 0)
    depth = jnp.where(depth < HALF, depth, depth - N).astype(f32)
    kinetic = (2.0 / float(N * N)) * (depth * depth) + plane_kinetic[...]
    spectrum = depth_product(matrix[...], returned[...])
    first = core[0] == 0
    for part in range(2):
        rows = slice(part * N, part * N + N)
        values = spectrum[rows] + kinetic * trial[rows, :]
        result[rows, :] = values
        away[part * HALF : part * HALF + HALF, :] = jnp.where(first, values[HALF:N], values[0:HALF])


def gram_kernel(core, result, brought, basis_all, gram, basis, own_sums, other_sums, sems):
    chips = basis_all.shape[0]

    def fetch(m):
        return pltpu.make_async_copy(basis_all.at[m], basis.at[m], sems.at[m])

    for m in range(chips):
        fetch(m).start()
    half = core[0] * HALF

    def one_chip(m, carry):
        fetch(m).wait()
        chip = jnp.where(m < chips // 2, 2 * m, 2 * chips - 1 - 2 * m)

        def rows(t, totals):
            totals = list(totals)
            row = pl.multiple_of(t * 8, 8)
            here = (pl.ds(row, 8), pl.ds(row + HALF, 8))
            mine = (pl.ds(pl.multiple_of(half + row, 8), 8), pl.ds(pl.multiple_of(half + N + row, 8), 8))
            for j in range(COLS // 128):
                tile = slice(j * 128, (j + 1) * 128)
                rights = [(result[mine[0], tile], result[mine[1], tile]), (brought[here[0], tile], brought[here[1], tile])]
                for slot in range(2):
                    left_real, left_imag = basis[m, slot, here[0], tile], basis[m, slot, here[1], tile]
                    for n, (real, imag) in enumerate(rights):
                        at = n * 4 + slot * 2
                        totals[at] = totals[at] + (left_real * real + left_imag * imag)
                        totals[at + 1] = totals[at + 1] + (left_real * imag - left_imag * real)
            return tuple(totals)

        totals = lax.fori_loop(0, HALF // 8, rows, (jnp.zeros((8, 128), f32),) * 8)
        for at in range(4):
            own_sums[pl.ds(chip * 4 + at, 1), :] = jnp.sum(totals[at], axis=0, keepdims=True)
            other_sums[pl.ds(chip * 4 + at, 1), :] = jnp.sum(totals[4 + at], axis=0, keepdims=True)
        return carry

    lax.fori_loop(0, chips, one_chip, 0)
    ones = jnp.ones((8, 128), bf16)
    own = exact_dot(ones, split3(own_sums[...]), ((1,), (1,)))
    other = exact_dot(ones, split3(other_sums[...]), ((1,), (1,)))
    first = core[0] == 0
    gram[0:8, :] = jnp.where(first, own, other)
    gram[8:16, :] = jnp.where(first, other, own)


def forward_kernel(
    site_row, box_base, recv, first_matrix, second_matrix, atoms, potential_in, beta_in,
    applied, shared, grid, mixed, stage, sums, potential, beta, sems,
):
    potential_copy = pltpu.make_async_copy(potential_in, potential, sems.at[0])
    beta_copy = pltpu.make_async_copy(beta_in, beta, sems.at[1])
    potential_copy.start()
    beta_copy.start()

    def transpose(d, carry):
        for j in range(COLS // 128):
            block = recv[d, :, j * 128 : (j + 1) * 128]
            real, imag, rest = block[0:16], block[16:32], block[32:40]
            swapped = pltpu.roll(rest, 4, 0)
            zero = jnp.zeros((8, 128), f32)
            stacked = jnp.concatenate(
                [real, rest, zero, real, rest, zero, imag, swapped, zero, imag, swapped, zero], axis=0
            )
            stage[pl.ds(pl.multiple_of(d * COLS + j * 128, 128), 128), :] = stacked.T
        return carry

    lax.fori_loop(0, N_GA, transpose, 0)

    def clear(t, carry):
        grid[pl.ds(pl.multiple_of(t * 256, 256), 256), :] = jnp.zeros((256, 128), f32)
        return carry

    lax.fori_loop(0, N * N // 256, clear, 0)

    def place(t, carry):
        base = t * 64
        for k in range(64):
            grid[pl.ds(site_row[base + k], 1), :] = stage[pl.ds(base + k, 1), :]
        return carry

    lax.fori_loop(0, NCOL // 64, place, 0)

    odd = (lanes() // 32) % 2 == 1

    def along_x(t, carry):
        blocks = []
        for k in range(GROUP):
            start = pl.multiple_of((t * GROUP + k) * 2 * N, 16)
            even_y = grid[pl.ds(start, N), :]
            odd_y = grid[pl.ds(start + N, N), :]
            blocks.append(jnp.where(odd, odd_y, even_y))
        result = fourier_rows(first_matrix[...], blocks)
        for k in range(GROUP):
            mixed[pl.ds((t * GROUP + k) * PITCH, N), :] = result[:, k * 128 : (k + 1) * 128]
        return carry

    lax.fori_loop(0, HALF // GROUP, along_x, 0)
    potential_copy.wait()

    def along_y(t, carry):
        blocks = []
        for k in range(GROUP):
            pair = t * GROUP + k
            blocks.append(
                exchange_pairs(
                    mixed[pl.ds(2 * pair, HALF, stride=PITCH), :], mixed[pl.ds(2 * pair + 1, HALF, stride=PITCH), :]
                )
            )
        result = fourier_rows(second_matrix[...], blocks)
        for k in range(GROUP):
            pair = t * GROUP + k
            values = result[:, k * 128 : (k + 1) * 128]
            start = pl.multiple_of(pair * ROWS_X, 8)
            grid[pl.ds(start, N), :] = values
            grid[pl.ds(start + N, 8), :] = values[0:8]
            applied[pl.ds(start, N), :] = values * potential[pl.ds(pl.multiple_of(pair * N, 16), N), :]
            applied[pl.ds(start + N, 8), :] = jnp.zeros((8, 128), f32)
        return carry

    for t in range(HALF // GROUP):
        along_y(t, 0)
    beta_copy.wait()

    def project(t, carry):
        for k in range(4):
            s = t * 4 + k
            total = jnp.zeros((8, 128), f32)
            for i, place in enumerate(box_places(box_base, s)):
                weight = beta[pl.ds(pl.multiple_of(s * 40 + i * 8, 8), 8), :]
                total = total + weight * grid[place, :]
            sums[pl.ds(pl.multiple_of(s * 8, 8), 8), :] = total
        return carry

    lax.fori_loop(0, SLOTS // 4, project, 0)
    totals = jnp.sum(sums[...].reshape(SLOTS, 8, 128), axis=1)
    row = lax.broadcasted_iota(jnp.int32, (8, 128), 0)
    column = lax.broadcasted_iota(jnp.int32, (8, 128), 1)
    chooser = jnp.where(row == column // 64, 1.0, 0.0).astype(bf16)
    partial = exact_dot(chooser, split3(totals), ((1,), (1,)))
    by_atom = exact_dot(split3(partial), atom_table(atoms), ((1,), (1,)))
    for part in range(2):
        for r in range(4):
            values = by_atom[part : part + 1, r * 256 : (r + 1) * 256]
            for d in range(N_GA):
                shared[d, part * 4 + r : part * 4 + r + 1, :] = values


def backward_kernel(
    site_row, box_base, shared, strength, atoms, first_matrix, second_matrix, parity, applied_in, beta_in,
    sent, applied, mixed, grid, stage, beta, weights, sems,
):
    beta_copy = pltpu.make_async_copy(beta_in, beta, sems.at[0])
    beta_copy.start()
    total = jnp.sum(shared[...], axis=0)
    by_part = []
    for part in range(2):
        whole_row = jnp.concatenate([total[part * 4 + r : part * 4 + r + 1, :] for r in range(4)], axis=1)
        by_part.append(jnp.broadcast_to(whole_row * strength[...], (64, ATOMS)))
    spread = jnp.concatenate(by_part, axis=0)
    weights[...] = exact_dot(split3(spread), atom_table(atoms), ((1,), (0,))).T
    beta_copy.wait()

    def add_boxes(t, carry):
        for k in range(2):
            s = t * 2 + k
            weight = weights[pl.ds(s, 1), :]
            places = box_places(box_base, s)
            olds = [applied[place, :] for place in places]
            for i in range(5):
                applied[places[i], :] = olds[i] + beta[pl.ds(pl.multiple_of(s * 40 + i * 8, 8), 8), :] * weight
        return carry

    lax.fori_loop(0, SLOTS // 2, add_boxes, 0)

    def along_y(t, carry):
        blocks = []
        for k in range(GROUP):
            start = pl.multiple_of((t * GROUP + k) * ROWS_X, 8)
            top = applied[pl.ds(start, 8), :] + applied[pl.ds(start + N, 8), :]
            blocks.append(jnp.concatenate([top, applied[pl.ds(start + 8, N - 8), :]], axis=0))
        result = fourier_rows(first_matrix[...], blocks)
        for k in range(GROUP):
            mixed[pl.ds((t * GROUP + k) * PITCH, N), :] = result[:, k * 128 : (k + 1) * 128]
        return carry

    lax.fori_loop(0, HALF // GROUP, along_y, 0)

    def along_x(t, carry):
        blocks = []
        for k in range(GROUP):
            pair = t * GROUP + k
            blocks.append(
                exchange_pairs(
                    mixed[pl.ds(2 * pair, HALF, stride=PITCH), :], mixed[pl.ds(2 * pair + 1, HALF, stride=PITCH), :]
                )
            )
        result = fourier_rows(second_matrix[...], blocks)
        for k in range(GROUP):
            grid[pl.ds(pl.multiple_of((t * GROUP + k) * N, 16), N), :] = result[:, k * 128 : (k + 1) * 128]
        return carry

    lax.fori_loop(0, HALF // GROUP, along_x, 0)

    def pick(t, carry):
        base = t * 64
        for k in range(64):
            stage[pl.ds(base + k, 1), :] = grid[pl.ds(site_row[base + k], 1), :]
        return carry

    lax.fori_loop(0, NCOL // 64, pick, 0)
    upper = lax.broadcasted_iota(jnp.int32, (8, 128), 0) < 4

    def transpose(d, carry):
        for j in range(COLS // 128):
            turned = stage[pl.ds(pl.multiple_of(d * COLS + j * 128, 128), 128), :].T
            is_odd = parity[pl.ds(d * (COLS // 128) + j, 1), :] > 0
            real = jnp.where(is_odd, turned[32:56], turned[0:24])
            imag = jnp.where(is_odd, turned[96:120], turned[64:88])
            rest = jnp.where(upper, real[16:24], pltpu.roll(imag[16:24], 4, 0))
            sent[d, :, j * 128 : (j + 1) * 128] = jnp.concatenate([real[0:16], imag[0:16], rest], axis=0)
        return carry

    lax.fori_loop(0, N_GA, transpose, 0)


def whole(space=pltpu.VMEM):
    return pl.BlockSpec(memory_space=space)


def frequency(index):
    return jnp.where(index < HALF, index, index - N).astype(f32)


def on_device(trial_bands, basis_bands, column_sites, potential, box_cells, box_atom, box_beta, strength):
    forward_depth, backward_depth = depth_matrices()
    bands = lax.axis_size("band")
    core = lax.axis_index("band") % 2
    halves = basis_bands.reshape(2, 2, HALF, COLS)
    swap = [(i, i ^ 1) for i in range(bands)]
    kept = jnp.where(core == 0, halves[:, 0], halves[:, 1])
    given = jnp.where(core == 0, halves[:, 1], halves[:, 0])
    trial = trial_bands.reshape(2 * N, COLS)
    taken = lax.ppermute(given, "band", swap)
    depth = pl.pallas_call(
        depth_kernel,
        out_shape=jax.ShapeDtypeStruct((2 * N, COLS), f32),
        in_specs=[whole()] * 2,
        out_specs=whole(),
        compiler_params=pltpu.CompilerParams(vmem_limit_bytes=60 * MIB),
        cost_estimate=pl.CostEstimate(flops=2000000000, bytes_accessed=8000000, transcendentals=0),
        name="depth",
    )(jnp.asarray(forward_depth), trial)
    taken, depth = lax.optimization_barrier((taken, depth))
    block = jnp.where(core == 0, jnp.stack([kept, taken]), jnp.stack([taken, kept])).reshape(2, N, COLS)
    depth, block = lax.optimization_barrier((depth, block))
    chip_order = list(range(0, bands // 2, 2)) + list(range(bands // 2 - 1, 0, -2))
    rings = [[2 * chip + k for chip in chip_order] for k in range(2)]
    basis_all = lax.all_gather(block, "band", axis=0, axis_index_groups=rings)
    recv = lax.all_to_all(depth.reshape(N_GA, 40, COLS), "ga", split_axis=0, concat_axis=0, tiled=True)

    site_x = column_sites // N
    site_y = column_sites - site_x * N
    corner = box_cells[:, 0]
    corner_plane = corner // (N * N)
    in_plane = corner - corner_plane * (N * N)
    corner_x = in_plane // N
    box_base = (corner_x // 2) * ROWS_X + (in_plane - corner_x * N)
    pot, beta = pl.pallas_call(
        prepare_kernel,
        out_shape=(
            jax.ShapeDtypeStruct((HALF * N, 128), f32),
            jax.ShapeDtypeStruct((SLOTS * 40, 128), f32),
        ),
        in_specs=[whole(pltpu.SMEM)] * 2 + [whole()] * 2,
        out_specs=(whole(pl.ANY), whole(pl.ANY)),
        scratch_shapes=[
            pltpu.VMEM((HALF * N, 128), f32),
            pltpu.VMEM((SLOTS * 40, 128), f32),
            pltpu.SemaphoreType.DMA((6,)),
        ],
        compiler_params=pltpu.CompilerParams(vmem_limit_bytes=57 * MIB),
        cost_estimate=pl.CostEstimate(flops=0, bytes_accessed=14000000, transcendentals=0),
        name="prepare",
    )(corner_plane, corner_x % 2, potential, box_beta)
    row_count = HALF * ROWS_X
    applied, shared = pl.pallas_call(
        forward_kernel,
        out_shape=(
            pltpu.VMEM((row_count, 128), f32),
            jax.ShapeDtypeStruct((N_GA, 8, ATOMS // 4), f32),
        ),
        in_specs=[whole(pltpu.SMEM)] * 2 + [whole()] * 4 + [whole(pl.ANY)] * 2,
        out_specs=(whole(), whole()),
        scratch_shapes=[
            pltpu.VMEM((N * N, 128), f32),
            pltpu.VMEM((HALF * PITCH, 128), f32),
            pltpu.VMEM((NCOL, 128), f32),
            pltpu.VMEM((SLOTS * 8, 128), f32),
            pltpu.VMEM((HALF * N, 128), f32),
            pltpu.VMEM((SLOTS * 40, 128), f32),
            pltpu.SemaphoreType.DMA((2,)),
        ],
        compiler_params=pltpu.CompilerParams(vmem_limit_bytes=50 * MIB),
        name="planes_forward",
    )(
        site_y * N + site_x,
        box_base,
        recv,
        jnp.asarray(stage_matrix(1.0, False)),
        jnp.asarray(stage_matrix(1.0, True)),
        box_atom.reshape(1, SLOTS),
        pot,
        beta,
    )
    shared = lax.all_to_all(shared, "ga", split_axis=0, concat_axis=0, tiled=True)
    sent, _ = pl.pallas_call(
        backward_kernel,
        out_shape=(jax.ShapeDtypeStruct((N_GA, 40, COLS), f32), pltpu.VMEM((row_count, 128), f32)),
        in_specs=[whole(pltpu.SMEM)] * 2 + [whole()] * 7 + [whole(pl.ANY)],
        out_specs=(whole(), whole()),
        input_output_aliases={8: 1},
        scratch_shapes=[
            pltpu.VMEM((HALF * PITCH, 128), f32),
            pltpu.VMEM((HALF * N, 128), f32),
            pltpu.VMEM((NCOL, 128), f32),
            pltpu.VMEM((SLOTS * 40, 128), f32),
            pltpu.VMEM((SLOTS, 128), f32),
            pltpu.SemaphoreType.DMA((1,)),
        ],
        compiler_params=pltpu.CompilerParams(vmem_limit_bytes=44 * MIB),
        name="planes_backward",
    )(
        (site_y // 2) * N + site_x,
        box_base,
        shared,
        strength.reshape(1, ATOMS),
        box_atom.reshape(1, SLOTS),
        jnp.asarray(stage_matrix(-1.0, False)),
        jnp.asarray(stage_matrix(-1.0, True)),
        (site_y % 2).reshape(NCOL // 128, 128),
        applied,
        beta,
    )
    returned = lax.all_to_all(sent, "ga", split_axis=0, concat_axis=0, tiled=True)
    own = lax.dynamic_slice_in_dim(column_sites, lax.axis_index("ga") * COLS, COLS)
    plane_kinetic = (2.0 / float(N * N)) * (frequency(own // N) ** 2 + frequency(own % N) ** 2)
    core_number = core.reshape(1)
    result, away = pl.pallas_call(
        finish_kernel,
        out_shape=(jax.ShapeDtypeStruct((2 * N, COLS), f32), jax.ShapeDtypeStruct((N, COLS), f32)),
        in_specs=[whole(pltpu.SMEM)] + [whole()] * 4,
        out_specs=(whole(), whole()),
        compiler_params=pltpu.CompilerParams(vmem_limit_bytes=24 * MIB),
        name="finish",
    )(
        core_number,
        jnp.asarray(backward_depth),
        returned.reshape(2 * N, COLS),
        trial,
        plane_kinetic.reshape(1, COLS),
    )
    brought = lax.ppermute(away, "band", swap)
    gram = pl.pallas_call(
        gram_kernel,
        out_shape=jax.ShapeDtypeStruct((16, 2 * bands), f32),
        in_specs=[whole(pltpu.SMEM)] + [whole()] * 2 + [whole(pl.ANY)],
        out_specs=whole(),
        scratch_shapes=[
            pltpu.VMEM((bands // 2, 2, N, COLS), f32),
            pltpu.VMEM((2 * bands, 128), f32),
            pltpu.VMEM((2 * bands, 128), f32),
            pltpu.SemaphoreType.DMA((bands // 2,)),
        ],
        compiler_params=pltpu.CompilerParams(vmem_limit_bytes=60 * MIB),
        name="gram",
    )(core_number, result, brought, basis_all)
    chip_group = [[(2 * chip + k) * N_GA + g for k in range(2) for g in range(N_GA)] for chip in range(bands // 2)]
    gram = lax.all_to_all(
        gram, ("band", "ga"), split_axis=0, concat_axis=0, tiled=True, axis_index_groups=chip_group
    )
    gram = (jnp.sum(gram, axis=0) * (1.0 / math.sqrt(N * NCOL))).reshape(bands, 2).T
    return (result.reshape(trial_bands.shape), gram[:, :, None])


def solution(mesh):
    placed = (
        P("band", None, None, "ga"),
        P("band", None, None, "ga"),
        P(),
        P("ga", None, None),
        P("ga", None),
        P("ga"),
        P("ga", None),
        P(),
    )
    return jax.shard_map(
        on_device,
        mesh=mesh,
        in_specs=placed,
        out_specs=(P("band", None, None, "ga"), P(None, None, "band")),
        check_vma=False,
    )
```

```python
import math

import jax
import jax.numpy as jnp
import numpy as np
from jax import lax
from jax.experimental import pallas as pl
from jax.experimental.pallas import tpu as pltpu
from jax.sharding import PartitionSpec as P

N = 160
HALF = N // 2
N_GA = 8
PLANES = N // N_GA
NCOL = 5120
COLS = NCOL // N_GA
SLOTS = 192
ROWS_X = N + 8
ATOMS = 1024
GROUP = 40
PITCH = 164
MIB = 1024 * 1024
bf16 = jnp.bfloat16
f32 = jnp.float32


def split_np(matrix):
    high = np.asarray(matrix, np.float32).astype(jnp.bfloat16)
    low = (np.asarray(matrix, np.float64) - high.astype(np.float64)).astype(np.float32).astype(jnp.bfloat16)
    return high, low


def fourier(orient):
    index = np.arange(N)
    angle = (np.outer(index, index) % N) * (2.0 * np.pi / N)
    return np.cos(angle), orient * np.sin(angle)


def stage_matrix(orient, paired):
    cosine, sine = fourier(orient)
    if paired:
        order = np.concatenate([np.arange(0, N, 2), np.arange(1, N, 2)])
        cosine, sine = cosine[:, order], sine[:, order]
    ch, cl = split_np(cosine)
    sh, sl = split_np(sine)
    return np.concatenate([ch, sh, ch, sh, cl, sl], axis=1)


def sent_order():
    rows = []
    for d in range(N_GA):
        for part, span in ((0, range(16)), (1, range(16)), (0, range(16, 20)), (1, range(16, 20))):
            rows += [(part, d * PLANES + p) for p in span]
    return rows


def depth_matrices():
    cosine, sine = fourier(1.0)
    full = np.block([[cosine, -sine], [sine, cosine]])
    back = np.block([[cosine, sine], [-sine, cosine]]) / float(N**3)
    order = np.array([part * N + z for part, z in sent_order()])
    tables = []
    for matrix in (full[order], back[:, order]):
        high, low = split_np(matrix)
        tables.append(np.concatenate([high, high, low], axis=1))
    return tables


def lanes():
    return lax.broadcasted_iota(jnp.int32, (1, 128), 1)


def fourier_rows(matrix, blocks):
    lane = lanes()
    sign = jnp.where(lane < 64, -1.0, 1.0).astype(f32)
    pieces = []
    for block in blocks:
        turned = pltpu.roll(block, 64, 1) * sign
        high = block.astype(bf16)
        low = (block - high.astype(f32)).astype(bf16)
        turned_high = turned.astype(bf16)
        turned_low = (turned - turned_high.astype(f32)).astype(bf16)
        pieces.append(jnp.concatenate([high, turned_high, low, turned_low, high, turned_high], axis=0))
    right = pieces[0] if len(pieces) == 1 else jnp.concatenate(pieces, axis=1)
    return jnp.dot(matrix, right, preferred_element_type=f32)


def exchange_pairs(first, second):
    odd = (lanes() // 32) % 2 == 1
    even_rows = jnp.where(odd, pltpu.roll(second, 32, 1), first)
    odd_rows = jnp.where(odd, second, pltpu.roll(first, 96, 1))
    return jnp.concatenate([even_rows, odd_rows], axis=0)


def split3(values):
    high = values.astype(bf16)
    rest = values - high.astype(f32)
    middle = rest.astype(bf16)
    return high, middle, (rest - middle.astype(f32)).astype(bf16)


def exact_dot(first, second, contract):
    total = None
    if isinstance(first, tuple):
        terms = [(piece, second) for piece in first]
    else:
        terms = [(first, piece) for piece in second]
    for left, right in terms:
        product = lax.dot_general(left, right, (contract, ((), ())), preferred_element_type=f32)
        total = product if total is None else total + product
    return total


def atom_table(atoms):
    row = lax.broadcasted_iota(jnp.int32, (ATOMS, SLOTS), 0)
    return jnp.where(atoms[...] == row, 1.0, 0.0).astype(bf16)


def box_places(box_base, s):
    places = []
    for i in range(5):
        start = box_base[s] + i * ROWS_X
        places.append(pl.ds(jnp.where(start >= HALF * ROWS_X, start - HALF * ROWS_X, start), 8))
    return places


def depth_product(matrix, values):
    high = values.astype(bf16)
    low = (values - high.astype(f32)).astype(bf16)
    return jnp.dot(matrix, jnp.concatenate([high, low, high], axis=0), preferred_element_type=f32)


def depth_kernel(matrix, values, out):
    out[...] = depth_product(matrix[...], values[...])


def prepare_kernel(
    box_plane, box_odd, potential, box_beta, potential_out, beta_out, rows, table, sems
):
    copies = []

    def send(source, target, start, size):
        span = pl.ds(start, size)
        copies.append(pltpu.make_async_copy(source.at[span], target.at[span], sems.at[len(copies)]))
        copies[-1].start()

    lane = lanes()
    lane_odd = (lane // 32) % 2 == 1
    lane_plane = lane % 32
    local_box = lax.broadcasted_iota(jnp.int32, (16, 128), 0) % 8
    local_plane = lane_plane - lax.broadcasted_iota(jnp.int32, (16, 128), 0) // 8
    nothing = jnp.zeros((8, 128), f32)

    def spread(t, carry):
        values = box_beta[pl.ds(pl.multiple_of(t * 8, 8), 8), :]
        both = jnp.concatenate([values, pltpu.roll(values, 64, 1)], axis=0)
        high = both.astype(bf16).astype(f32)
        left = jnp.concatenate([high, both - high], axis=0).T[0:64].astype(bf16)
        masks = []
        for k in range(8):
            hit = (local_box == k) & (local_plane == box_plane[t * 8 + k])
            masks.append(jnp.where(hit, 1.0, 0.0))
        mask = jnp.concatenate(masks, axis=1)
        right = jnp.concatenate([mask, mask], axis=0).astype(bf16)
        lines = jnp.dot(left, right, preferred_element_type=f32)
        for k in range(8):
            s = t * 8 + k
            shifted = box_odd[s] > 0
            line = [lines[x * 8 : x * 8 + 8, k * 128 : (k + 1) * 128] for x in range(8)]
            for i in range(5):
                even = line[2 * i] if i < 4 else nothing
                straight = jnp.where(lane_odd, line[2 * i + 1], even) if i < 4 else nothing
                moved = jnp.where(lane_odd, even, line[2 * i - 1] if i > 0 else nothing)
                table[pl.ds(pl.multiple_of(s * 40 + i * 8, 8), 8), :] = jnp.where(shifted, moved, straight)
        return carry

    def spread_two(t, carry):
        spread(2 * t, 0)
        spread(2 * t + 1, 0)
        return carry

    for piece in range(2):
        lax.fori_loop(piece * 6, piece * 6 + 6, spread_two, 0)
        send(table, beta_out, piece * SLOTS * 20, SLOTS * 20)
    zero = jnp.zeros((8, N), f32)
    for piece in range(4):
        for k in range(HALF // 4):
            pair = piece * (HALF // 4) + k
            pieces = []
            for half in range(2):
                plane = potential[:, 2 * pair + half, :]
                pieces += [plane[0:8], plane[8:16], jnp.concatenate([plane[16:20], zero[0:4]], axis=0), zero]
            stacked = jnp.concatenate(pieces + pieces, axis=0)
            rows[pair * N : pair * N + 128, :] = stacked[:, 0:128].T
            rows[pair * N + 128 : pair * N + N, :] = stacked[:, 128:N].T
        send(rows, potential_out, piece * (HALF // 4) * N, (HALF // 4) * N)
    for copy in copies:
        copy.wait()


def finish_kernel(core, matrix, returned, trial, plane_kinetic, result, away):
    depth = lax.broadcasted_iota(jnp.int32, (N, 1), 0)
    depth = jnp.where(depth < HALF, depth, depth - N).astype(f32)
    kinetic = (2.0 / float(N * N)) * (depth * depth) + plane_kinetic[...]
    spectrum = depth_product(matrix[...], returned[...])
    first = core[0] == 0
    for part in range(2):
        rows = slice(part * N, part * N + N)
        values = spectrum[rows] + kinetic * trial[rows, :]
        result[rows, :] = values
        away[part * HALF : part * HALF + HALF, :] = jnp.where(first, values[HALF:N], values[0:HALF])


def gram_kernel(core, result, brought, basis_all, gram, basis, own_sums, other_sums, sems):
    chips = basis_all.shape[0]

    def fetch(m):
        return pltpu.make_async_copy(basis_all.at[m], basis.at[m], sems.at[m])

    for m in range(chips):
        fetch(m).start()
    half = core[0] * HALF

    def one_chip(m, carry):
        fetch(m).wait()
        chip = jnp.where(m < chips // 2, 2 * m, 2 * chips - 1 - 2 * m)

        def rows(t, totals):
            totals = list(totals)
            row = pl.multiple_of(t * 8, 8)
            here = (pl.ds(row, 8), pl.ds(row + HALF, 8))
            mine = (pl.ds(pl.multiple_of(half + row, 8), 8), pl.ds(pl.multiple_of(half + N + row, 8), 8))
            for j in range(COLS // 128):
                tile = slice(j * 128, (j + 1) * 128)
                rights = [(result[mine[0], tile], result[mine[1], tile]), (brought[here[0], tile], brought[here[1], tile])]
                for slot in range(2):
                    left_real, left_imag = basis[m, slot, here[0], tile], basis[m, slot, here[1], tile]
                    for n, (real, imag) in enumerate(rights):
                        at = n * 4 + slot * 2
                        totals[at] = totals[at] + (left_real * real + left_imag * imag)
                        totals[at + 1] = totals[at + 1] + (left_real * imag - left_imag * real)
            return tuple(totals)

        totals = lax.fori_loop(0, HALF // 8, rows, (jnp.zeros((8, 128), f32),) * 8)
        for at in range(4):
            own_sums[pl.ds(chip * 4 + at, 1), :] = jnp.sum(totals[at], axis=0, keepdims=True)
            other_sums[pl.ds(chip * 4 + at, 1), :] = jnp.sum(totals[4 + at], axis=0, keepdims=True)
        return carry

    lax.fori_loop(0, chips, one_chip, 0)
    ones = jnp.ones((8, 128), bf16)
    own = exact_dot(ones, split3(own_sums[...]), ((1,), (1,)))
    other = exact_dot(ones, split3(other_sums[...]), ((1,), (1,)))
    first = core[0] == 0
    gram[0:8, :] = jnp.where(first, own, other)
    gram[8:16, :] = jnp.where(first, other, own)


def forward_kernel(
    site_row, box_base, recv, first_matrix, second_matrix, atoms, potential_in, beta_in,
    applied, shared, grid, mixed, stage, sums, potential, beta, sems,
):
    potential_copy = pltpu.make_async_copy(potential_in, potential, sems.at[0])
    beta_copy = pltpu.make_async_copy(beta_in, beta, sems.at[1])
    potential_copy.start()
    beta_copy.start()

    def transpose(d, carry):
        for j in range(COLS // 128):
            block = recv[d, :, j * 128 : (j + 1) * 128]
            real, imag, rest = block[0:16], block[16:32], block[32:40]
            swapped = pltpu.roll(rest, 4, 0)
            zero = jnp.zeros((8, 128), f32)
            stacked = jnp.concatenate(
                [real, rest, zero, real, rest, zero, imag, swapped, zero, imag, swapped, zero], axis=0
            )
            stage[pl.ds(pl.multiple_of(d * COLS + j * 128, 128), 128), :] = stacked.T
        return carry

    lax.fori_loop(0, N_GA, transpose, 0)

    def clear(t, carry):
        grid[pl.ds(pl.multiple_of(t * 256, 256), 256), :] = jnp.zeros((256, 128), f32)
        return carry

    lax.fori_loop(0, N * N // 256, clear, 0)

    def place(t, carry):
        base = t * 64
        for k in range(64):
            grid[pl.ds(site_row[base + k], 1), :] = stage[pl.ds(base + k, 1), :]
        return carry

    lax.fori_loop(0, NCOL // 64, place, 0)

    odd = (lanes() // 32) % 2 == 1

    def along_x(t, carry):
        blocks = []
        for k in range(GROUP):
            start = pl.multiple_of((t * GROUP + k) * 2 * N, 16)
            even_y = grid[pl.ds(start, N), :]
            odd_y = grid[pl.ds(start + N, N), :]
            blocks.append(jnp.where(odd, odd_y, even_y))
        result = fourier_rows(first_matrix[...], blocks)
        for k in range(GROUP):
            mixed[pl.ds((t * GROUP + k) * PITCH, N), :] = result[:, k * 128 : (k + 1) * 128]
        return carry

    lax.fori_loop(0, HALF // GROUP, along_x, 0)
    potential_copy.wait()

    def along_y(t, carry):
        blocks = []
        for k in range(GROUP):
            pair = t * GROUP + k
            blocks.append(
                exchange_pairs(
                    mixed[pl.ds(2 * pair, HALF, stride=PITCH), :], mixed[pl.ds(2 * pair + 1, HALF, stride=PITCH), :]
                )
            )
        result = fourier_rows(second_matrix[...], blocks)
        for k in range(GROUP):
            pair = t * GROUP + k
            values = result[:, k * 128 : (k + 1) * 128]
            start = pl.multiple_of(pair * ROWS_X, 8)
            grid[pl.ds(start, N), :] = values
            grid[pl.ds(start + N, 8), :] = values[0:8]
            applied[pl.ds(start, N), :] = values * potential[pl.ds(pl.multiple_of(pair * N, 16), N), :]
            applied[pl.ds(start + N, 8), :] = jnp.zeros((8, 128), f32)
        return carry

    for t in range(HALF // GROUP):
        along_y(t, 0)
    beta_copy.wait()

    def project(t, carry):
        for k in range(4):
            s = t * 4 + k
            total = jnp.zeros((8, 128), f32)
            for i, place in enumerate(box_places(box_base, s)):
                weight = beta[pl.ds(pl.multiple_of(s * 40 + i * 8, 8), 8), :]
                total = total + weight * grid[place, :]
            sums[pl.ds(pl.multiple_of(s * 8, 8), 8), :] = total
        return carry

    lax.fori_loop(0, SLOTS // 4, project, 0)
    totals = jnp.sum(sums[...].reshape(SLOTS, 8, 128), axis=1)
    row = lax.broadcasted_iota(jnp.int32, (8, 128), 0)
    column = lax.broadcasted_iota(jnp.int32, (8, 128), 1)
    chooser = jnp.where(row == column // 64, 1.0, 0.0).astype(bf16)
    partial = exact_dot(chooser, split3(totals), ((1,), (1,)))
    by_atom = exact_dot(split3(partial), atom_table(atoms), ((1,), (1,)))
    for part in range(2):
        for r in range(4):
            values = by_atom[part : part + 1, r * 256 : (r + 1) * 256]
            for d in range(N_GA):
                shared[d, part * 4 + r : part * 4 + r + 1, :] = values


def backward_kernel(
    site_row, box_base, shared, strength, atoms, first_matrix, second_matrix, parity, applied_in, beta_in,
    sent, applied, mixed, grid, stage, beta, weights, sems,
):
    beta_copy = pltpu.make_async_copy(beta_in, beta, sems.at[0])
    beta_copy.start()
    total = jnp.sum(shared[...], axis=0)
    by_part = []
    for part in range(2):
        whole_row = jnp.concatenate([total[part * 4 + r : part * 4 + r + 1, :] for r in range(4)], axis=1)
        by_part.append(jnp.broadcast_to(whole_row * strength[...], (64, ATOMS)))
    spread = jnp.concatenate(by_part, axis=0)
    weights[...] = exact_dot(split3(spread), atom_table(atoms), ((1,), (0,))).T
    beta_copy.wait()

    def add_boxes(t, carry):
        for k in range(4):
            s = t * 4 + k
            weight = weights[pl.ds(s, 1), :]
            places = box_places(box_base, s)
            olds = [applied[place, :] for place in places]
            for i in range(5):
                applied[places[i], :] = olds[i] + beta[pl.ds(pl.multiple_of(s * 40 + i * 8, 8), 8), :] * weight
        return carry

    lax.fori_loop(0, SLOTS // 4, add_boxes, 0)

    def along_y(t, carry):
        blocks = []
        for k in range(GROUP):
            start = pl.multiple_of((t * GROUP + k) * ROWS_X, 8)
            top = applied[pl.ds(start, 8), :] + applied[pl.ds(start + N, 8), :]
            blocks.append(jnp.concatenate([top, applied[pl.ds(start + 8, N - 8), :]], axis=0))
        result = fourier_rows(first_matrix[...], blocks)
        for k in range(GROUP):
            mixed[pl.ds((t * GROUP + k) * PITCH, N), :] = result[:, k * 128 : (k + 1) * 128]
        return carry

    lax.fori_loop(0, HALF // GROUP, along_y, 0)

    def along_x(t, carry):
        blocks = []
        for k in range(GROUP):
            pair = t * GROUP + k
            blocks.append(
                exchange_pairs(
                    mixed[pl.ds(2 * pair, HALF, stride=PITCH), :], mixed[pl.ds(2 * pair + 1, HALF, stride=PITCH), :]
                )
            )
        result = fourier_rows(second_matrix[...], blocks)
        for k in range(GROUP):
            grid[pl.ds(pl.multiple_of((t * GROUP + k) * N, 16), N), :] = result[:, k * 128 : (k + 1) * 128]
        return carry

    lax.fori_loop(0, HALF // GROUP, along_x, 0)

    def pick(t, carry):
        base = t * 64
        for k in range(64):
            stage[pl.ds(base + k, 1), :] = grid[pl.ds(site_row[base + k], 1), :]
        return carry

    lax.fori_loop(0, NCOL // 64, pick, 0)
    upper = lax.broadcasted_iota(jnp.int32, (8, 128), 0) < 4

    def transpose(d, carry):
        for j in range(COLS // 128):
            turned = stage[pl.ds(pl.multiple_of(d * COLS + j * 128, 128), 128), :].T
            is_odd = parity[pl.ds(d * (COLS // 128) + j, 1), :] > 0
            real = jnp.where(is_odd, turned[32:56], turned[0:24])
            imag = jnp.where(is_odd, turned[96:120], turned[64:88])
            rest = jnp.where(upper, real[16:24], pltpu.roll(imag[16:24], 4, 0))
            sent[d, :, j * 128 : (j + 1) * 128] = jnp.concatenate([real[0:16], imag[0:16], rest], axis=0)
        return carry

    lax.fori_loop(0, N_GA, transpose, 0)


def whole(space=pltpu.VMEM):
    return pl.BlockSpec(memory_space=space)


def frequency(index):
    return jnp.where(index < HALF, index, index - N).astype(f32)


def on_device(trial_bands, basis_bands, column_sites, potential, box_cells, box_atom, box_beta, strength):
    forward_depth, backward_depth = depth_matrices()
    bands = lax.axis_size("band")
    core = lax.axis_index("band") % 2
    halves = basis_bands.reshape(2, 2, HALF, COLS)
    swap = [(i, i ^ 1) for i in range(bands)]
    kept = jnp.where(core == 0, halves[:, 0], halves[:, 1])
    given = jnp.where(core == 0, halves[:, 1], halves[:, 0])
    trial = trial_bands.reshape(2 * N, COLS)
    taken = lax.ppermute(given, "band", swap)
    depth = pl.pallas_call(
        depth_kernel,
        out_shape=jax.ShapeDtypeStruct((2 * N, COLS), f32),
        in_specs=[whole()] * 2,
        out_specs=whole(),
        compiler_params=pltpu.CompilerParams(vmem_limit_bytes=60 * MIB),
        cost_estimate=pl.CostEstimate(flops=2000000000, bytes_accessed=8000000, transcendentals=0),
        name="depth",
    )(jnp.asarray(forward_depth), trial)
    taken, depth = lax.optimization_barrier((taken, depth))
    block = jnp.where(core == 0, jnp.stack([kept, taken]), jnp.stack([taken, kept])).reshape(2, N, COLS)
    depth, block = lax.optimization_barrier((depth, block))
    chip_order = list(range(0, bands // 2, 2)) + list(range(bands // 2 - 1, 0, -2))
    rings = [[2 * chip + k for chip in chip_order] for k in range(2)]
    basis_all = lax.all_gather(block, "band", axis=0, axis_index_groups=rings)
    recv = lax.all_to_all(depth.reshape(N_GA, 40, COLS), "ga", split_axis=0, concat_axis=0, tiled=True)

    site_x = column_sites // N
    site_y = column_sites - site_x * N
    corner = box_cells[:, 0]
    corner_plane = corner // (N * N)
    in_plane = corner - corner_plane * (N * N)
    corner_x = in_plane // N
    box_base = (corner_x // 2) * ROWS_X + (in_plane - corner_x * N)
    pot, beta = pl.pallas_call(
        prepare_kernel,
        out_shape=(
            jax.ShapeDtypeStruct((HALF * N, 128), f32),
            jax.ShapeDtypeStruct((SLOTS * 40, 128), f32),
        ),
        in_specs=[whole(pltpu.SMEM)] * 2 + [whole()] * 2,
        out_specs=(whole(pl.ANY), whole(pl.ANY)),
        scratch_shapes=[
            pltpu.VMEM((HALF * N, 128), f32),
            pltpu.VMEM((SLOTS * 40, 128), f32),
            pltpu.SemaphoreType.DMA((6,)),
        ],
        compiler_params=pltpu.CompilerParams(vmem_limit_bytes=24 * MIB),
        cost_estimate=pl.CostEstimate(flops=0, bytes_accessed=14000000, transcendentals=0),
        name="prepare",
    )(corner_plane, corner_x % 2, potential, box_beta)
    row_count = HALF * ROWS_X
    applied, shared = pl.pallas_call(
        forward_kernel,
        out_shape=(
            pltpu.VMEM((row_count, 128), f32),
            jax.ShapeDtypeStruct((N_GA, 8, ATOMS // 4), f32),
        ),
        in_specs=[whole(pltpu.SMEM)] * 2 + [whole()] * 4 + [whole(pl.ANY)] * 2,
        out_specs=(whole(), whole()),
        scratch_shapes=[
            pltpu.VMEM((N * N, 128), f32),
            pltpu.VMEM((HALF * PITCH, 128), f32),
            pltpu.VMEM((NCOL, 128), f32),
            pltpu.VMEM((SLOTS * 8, 128), f32),
            pltpu.VMEM((HALF * N, 128), f32),
            pltpu.VMEM((SLOTS * 40, 128), f32),
            pltpu.SemaphoreType.DMA((2,)),
        ],
        compiler_params=pltpu.CompilerParams(vmem_limit_bytes=50 * MIB),
        name="planes_forward",
    )(
        site_y * N + site_x,
        box_base,
        recv,
        jnp.asarray(stage_matrix(1.0, False)),
        jnp.asarray(stage_matrix(1.0, True)),
        box_atom.reshape(1, SLOTS),
        pot,
        beta,
    )
    shared = lax.all_to_all(shared, "ga", split_axis=0, concat_axis=0, tiled=True)
    sent, _ = pl.pallas_call(
        backward_kernel,
        out_shape=(jax.ShapeDtypeStruct((N_GA, 40, COLS), f32), pltpu.VMEM((row_count, 128), f32)),
        in_specs=[whole(pltpu.SMEM)] * 2 + [whole()] * 7 + [whole(pl.ANY)],
        out_specs=(whole(), whole()),
        input_output_aliases={8: 1},
        scratch_shapes=[
            pltpu.VMEM((HALF * PITCH, 128), f32),
            pltpu.VMEM((HALF * N, 128), f32),
            pltpu.VMEM((NCOL, 128), f32),
            pltpu.VMEM((SLOTS * 40, 128), f32),
            pltpu.VMEM((SLOTS, 128), f32),
            pltpu.SemaphoreType.DMA((1,)),
        ],
        compiler_params=pltpu.CompilerParams(vmem_limit_bytes=44 * MIB),
        name="planes_backward",
    )(
        (site_y // 2) * N + site_x,
        box_base,
        shared,
        strength.reshape(1, ATOMS),
        box_atom.reshape(1, SLOTS),
        jnp.asarray(stage_matrix(-1.0, False)),
        jnp.asarray(stage_matrix(-1.0, True)),
        (site_y % 2).reshape(NCOL // 128, 128),
        applied,
        beta,
    )
    returned = lax.all_to_all(sent, "ga", split_axis=0, concat_axis=0, tiled=True)
    own = lax.dynamic_slice_in_dim(column_sites, lax.axis_index("ga") * COLS, COLS)
    plane_kinetic = (2.0 / float(N * N)) * (frequency(own // N) ** 2 + frequency(own % N) ** 2)
    core_number = core.reshape(1)
    result, away = pl.pallas_call(
        finish_kernel,
        out_shape=(jax.ShapeDtypeStruct((2 * N, COLS), f32), jax.ShapeDtypeStruct((N, COLS), f32)),
        in_specs=[whole(pltpu.SMEM)] + [whole()] * 4,
        out_specs=(whole(), whole()),
        compiler_params=pltpu.CompilerParams(vmem_limit_bytes=24 * MIB),
        name="finish",
    )(
        core_number,
        jnp.asarray(backward_depth),
        returned.reshape(2 * N, COLS),
        trial,
        plane_kinetic.reshape(1, COLS),
    )
    brought = lax.ppermute(away, "band", swap)
    gram = pl.pallas_call(
        gram_kernel,
        out_shape=jax.ShapeDtypeStruct((16, 2 * bands), f32),
        in_specs=[whole(pltpu.SMEM)] + [whole()] * 2 + [whole(pl.ANY)],
        out_specs=whole(),
        scratch_shapes=[
            pltpu.VMEM((bands // 2, 2, N, COLS), f32),
            pltpu.VMEM((2 * bands, 128), f32),
            pltpu.VMEM((2 * bands, 128), f32),
            pltpu.SemaphoreType.DMA((bands // 2,)),
        ],
        compiler_params=pltpu.CompilerParams(vmem_limit_bytes=60 * MIB),
        name="gram",
    )(core_number, result, brought, basis_all)
    chip_group = [[(2 * chip + k) * N_GA + g for k in range(2) for g in range(N_GA)] for chip in range(bands // 2)]
    gram = lax.all_to_all(
        gram, ("band", "ga"), split_axis=0, concat_axis=0, tiled=True, axis_index_groups=chip_group
    )
    gram = (jnp.sum(gram, axis=0) * (1.0 / math.sqrt(N * NCOL))).reshape(bands, 2).T
    return (result.reshape(trial_bands.shape), gram[:, :, None])


def solution(mesh):
    placed = (
        P("band", None, None, "ga"),
        P("band", None, None, "ga"),
        P(),
        P("ga", None, None),
        P("ga", None),
        P("ga"),
        P("ga", None),
        P(),
    )
    return jax.shard_map(
        on_device,
        mesh=mesh,
        in_specs=placed,
        out_specs=(P("band", None, None, "ga"), P(None, None, "band")),
        check_vma=False,
    )
```
